32 devices in a mesh: traj: 2 (over y), pair: 4 (over z), aux: 2 (over x), root: 2 (over core).
Axes of the slice: x: 2, y: 2, z: 4, core: 2. Of those that a mesh axis runs over, the one named last changes fastest.
Arguments:
- b_built: bfloat16 [4, 4, 1024, 2048], P(('traj', 'aux'), None, None, 'pair'), parts along dimension 0, may hold values from -0.0625 to 0.0625
- trial: bfloat16 [16384, 512], P(('traj', 'pair', 'aux'), 'root'), parts along dimension 0, may hold values from -6 to 6
- energy_gap: float32 [16384], P(('traj', 'pair', 'aux')), parts along dimension 0, may hold values from 0.3 to 3
- block_live: int32 [128], P(('traj', 'pair')), parts along dimension 0, may hold values from 0 to 1, as said below
Outputs:
- sigma_out: bfloat16 [16384, 512], P(('traj', 'pair', 'aux'), 'root'), parts along dimension 0
The draws below stay inside these ranges and needn't reach their ends.
There are 2 independent parts, one for each index of `traj`. The reference program is written for one: setup_inputs(seed, part) draws one part's arguments, and reference() takes and returns one part's arrays. A program takes and returns all parts, laid end to end along the dimension named above; each array names one. Nothing has to cross between parts.
Inputs may be any that keep to these rules, and one draw needn't show every extreme that they name: `block_live`: each pair index holds at most 10 screened-in blocks among its 16, one or more, and some pair index holds exactly 10.
All inputs are finite; a program needn't handle non-finite values.
Results may differ from the reference program's by a relative error of at most 0.0045.
Values may be sent and summed in bfloat16 or wider, within the bound.
No kernel may reach another device: no remote copies, remote signals or barrier semaphores. Data moves between devices by JAX's collectives and lax.ppermute only.
A program may use at most 64 MiB of HBM per device.

```python
import math
import jax
import jax.numpy as jnp
from jax import lax

BLK = 128
PB_DEV = 16
RP = 1024
NPB = 64
ROWS = 8192
AUX = 2048
VECS = 512
LIVE_MAX = 10
N_PAIR = 4
N_AUX = 2


def draw_block_live(key, part):
    key = jax.random.fold_in(key, 11)
    key = jax.random.fold_in(key, part)
    key_count, key_top, key_score = jax.random.split(key, 3)
    groups = NPB // PB_DEV
    counts = jax.random.randint(key_count, (groups,), 1, max(1, LIVE_MAX // 2) + 1)
    busiest = jax.random.randint(key_top, (), 0, groups)
    counts = jnp.where(jnp.arange(groups) == busiest, LIVE_MAX, counts)
    scores = jax.random.randint(key_score, (groups, PB_DEV), 0, 1 << 20) * PB_DEV + jnp.arange(PB_DEV)[None, :]
    ranks = jnp.argsort(jnp.argsort(scores, axis=1), axis=1)
    return (ranks < counts[:, None]).astype(jnp.int32).reshape(-1)


def level_of(key, extent, cuts, low, largest):
    factor_of, own = 1.0, jax.random.fold_in(key, 6)
    for axis_at, blocks in cuts:
        steps = jnp.exp(jax.random.uniform(jax.random.fold_in(own, axis_at), (blocks,), jnp.float32, low / len(cuts), largest / len(cuts)))
        factor_of = factor_of * jnp.repeat(steps, extent[axis_at] // blocks).reshape([-1 if axis == axis_at else 1 for axis in range(len(extent))])
    return factor_of


def scatter_about(own_key, dims, deviation, most, pieces=(), held_as=jnp.bfloat16):
    result = jax.random.normal(own_key, dims, jnp.float32) * deviation
    if len(pieces) > 0:
        result = level_of(own_key, dims, pieces, -0.22, 0.18) * result
    return jnp.clip(result, min=-most, max=most).astype(held_as)


def setup_inputs(seed: int = 0, part: int = 0) -> dict:
    key_of = jax.random.split(jax.random.key(seed), 5)
    own_keys = jax.random.split(jax.random.fold_in(key_of[4], part), 5)
    b_built = scatter_about(own_keys[0], (N_AUX, N_PAIR, RP, AUX), (ROWS + AUX) ** -0.5, 0.0625, ((0, 2), (3, 4)))
    trial = scatter_about(own_keys[1], (ROWS, VECS), 1.0, 6.0, ((0, 8), (1, 2)))
    energy_gap = jnp.clip(jnp.exp(math.log(3.0) - 2.3025851 * jax.random.uniform(own_keys[2], (ROWS,), jnp.float32) ** level_of(own_keys[2], (ROWS,), ((0, 8),), -0.2, 0.2)), 0.3, 3.0)
    block_live = draw_block_live(jax.random.fold_in(jax.random.fold_in(key_of[4], part), 71), part)
    return dict(b_built=b_built, trial=trial, energy_gap=energy_gap, block_live=block_live)


def reference(b_built, trial, energy_gap, block_live):
    b_full = jnp.transpose(b_built, (1, 0, 2, 3)).reshape(-1, b_built.shape[3])
    live_rows = jnp.repeat(block_live, BLK).astype(jnp.bfloat16)[:, None]
    masked = trial * live_rows
    coeffs = lax.dot_general(b_full, masked, (((0,), (0,)), ((), ())), preferred_element_type=jnp.float32).astype(jnp.bfloat16)
    response = jnp.dot(b_full, coeffs, preferred_element_type=jnp.float32)
    sigma_out = energy_gap[:, None] * trial.astype(jnp.float32) + 2.0 * live_rows.astype(jnp.float32) * response
    return sigma_out.astype(jnp.bfloat16)
```

```python
import jax
import jax.numpy as jnp
from jax import lax
from jax.sharding import PartitionSpec as P

BLK = 128
V_PARTS = 2


def contract_rows(left, right):
    return lax.dot_general(
        left, right, (((0,), (0,)), ((), ())), preferred_element_type=jnp.float32
    )


def exchange_sum(partial, n_aux):
    sent = partial.astype(jnp.bfloat16)
    if n_aux == 1:
        return sent
    if n_aux == 2:
        other = lax.ppermute(sent, "aux", [(0, 1), (1, 0)])
        return (partial + other.astype(jnp.float32)).astype(jnp.bfloat16)
    return lax.psum(sent, "aux")


def body(n_pair, n_aux, b_built, trial, energy_gap, block_live):
    rows, vecs = trial.shape
    blocks = rows // BLK
    me = lax.axis_index("pair")
    own_blocks = lax.dynamic_slice_in_dim(block_live, lax.axis_index("aux") * blocks, blocks, 0)
    own_live = jnp.repeat(own_blocks, BLK)
    masked = trial * own_live.astype(jnp.bfloat16)[:, None]
    factors = b_built[0]

    def factor(pair):
        return lax.dynamic_index_in_dim(factors, pair, 0, keepdims=False)

    up = {k: [(z, z + 1) for z in range(k - 1, n_pair - 1)] for k in range(1, n_pair)}
    down = {k: [(z, z - 1) for z in range(n_pair - k, 0, -1)] for k in range(1, n_pair)}

    width = vecs // V_PARTS
    outs = []
    for part in range(V_PARTS):
        own = masked[:, part * width : (part + 1) * width]
        partial = contract_rows(factor(me), own)
        from_below, from_above = {0: own}, {0: own}
        for k in range(1, n_pair):
            from_below[k] = lax.ppermute(from_below[k - 1], "pair", up[k])
            from_above[k] = lax.ppermute(from_above[k - 1], "pair", down[k])
        for k in range(1, n_pair):
            got = from_below[k] + from_above[n_pair - k]
            partial = partial + contract_rows(factor((me - k) % n_pair), got)
        coeffs = exchange_sum(partial, n_aux)

        def share(pair):
            return jnp.dot(factor(pair), coeffs, preferred_element_type=jnp.float32)

        shares = {k: share((me + k) % n_pair) for k in range(n_pair)}
        going_up = going_down = None
        for k in range(n_pair - 1, 0, -1):
            rise, fall = shares[k], shares[n_pair - k]
            if going_up is not None:
                rise = rise + going_up.astype(jnp.float32)
                fall = fall + going_down.astype(jnp.float32)
            going_up = lax.ppermute(
                rise.astype(jnp.bfloat16), "pair", [(z, z + 1) for z in range(0, n_pair - k)]
            )
            going_down = lax.ppermute(
                fall.astype(jnp.bfloat16), "pair", [(z, z - 1) for z in range(n_pair - 1, k - 1, -1)]
            )
        response = shares[0] + going_up.astype(jnp.float32) + going_down.astype(jnp.float32)
        outs.append(response)
    response = jnp.concatenate(outs, axis=1)
    sigma_out = (
        energy_gap[:, None] * trial.astype(jnp.float32)
        + 2.0 * own_live.astype(jnp.float32)[:, None] * response
    )
    return sigma_out.astype(jnp.bfloat16)


def solution(mesh):
    n_pair, n_aux = mesh.shape["pair"], mesh.shape["aux"]
    return jax.shard_map(
        lambda *args: body(n_pair, n_aux, *args),
        mesh=mesh,
        in_specs=(
            P(("traj", "aux"), None, None, "pair"),
            P(("traj", "pair", "aux"), "root"),
            P(("traj", "pair", "aux")),
            P(("traj", "pair")),
        ),
        out_specs=P(("traj", "pair", "aux"), "root"),
        check_vma=False,
    )
```

```python
import jax
import jax.numpy as jnp
from jax import lax
from jax.sharding import PartitionSpec as P

BLK = 128
V_PARTS = 2


def contract_rows(left, right):
    return lax.dot_general(
        left, right, (((0,), (0,)), ((), ())), preferred_element_type=jnp.float32
    )


def exchange_sum(partial, n_aux):
    sent = partial.astype(jnp.bfloat16)
    if n_aux == 1:
        return sent
    if n_aux == 2:
        other = lax.ppermute(sent, "aux", [(0, 1), (1, 0)])
        return (partial + other.astype(jnp.float32)).astype(jnp.bfloat16)
    return lax.psum(sent, "aux")


def along_line(masked, factors, n_aux):
    me = lax.axis_index("pair")
    middle = (me == 1) | (me == 2)

    def factor(flip):
        return lax.dynamic_index_in_dim(factors, me ^ flip, 0, keepdims=False)

    near = [(z, z ^ 1) for z in range(4)]
    far = [(z, z ^ 2) for z in range(4)]
    inner = [(1, 2), (2, 1)]
    outward = [(2, 3), (1, 0)]
    inward = [(3, 2), (0, 1)]

    width = masked.shape[1] // V_PARTS
    owns = [masked[:, part * width : (part + 1) * width] for part in range(V_PARTS)]
    outs = []
    for own in owns:
        from_far = lax.ppermute(own, "pair", far)
        from_near = lax.ppermute(own, "pair", near)
        from_inner = lax.ppermute(own, "pair", inner)
        from_outer = lax.ppermute(from_far, "pair", outward)
        opposite = jnp.where(middle, from_inner, from_outer)
        partial = contract_rows(own, factor(0))
        partial = partial + contract_rows(from_near, factor(1))
        partial = partial + contract_rows(from_far, factor(2))
        partial = partial + contract_rows(opposite, factor(3))
        coeffs = exchange_sum(partial, n_aux)

        def share(flip):
            return lax.dot_general(
                factor(flip), coeffs, (((1,), (1,)), ((), ())), preferred_element_type=jnp.float32
            )

        share_3 = share(3).astype(jnp.bfloat16)
        got_outer = lax.ppermute(share_3, "pair", inward)
        got_inner = lax.ppermute(share_3, "pair", inner)
        got_near = lax.ppermute(share(1).astype(jnp.bfloat16), "pair", near)
        onward = share(2) + got_outer.astype(jnp.float32)
        got_far = lax.ppermute(onward.astype(jnp.bfloat16), "pair", far)
        response = share(0)
        for got in (got_near, got_inner, got_far):
            response = response + got.astype(jnp.float32)
        outs.append(response)
    return jnp.concatenate(outs, axis=1)


def gathered(masked, factors, n_aux):
    everyone = lax.all_gather(masked, "pair", axis=0, tiled=True)
    rows = factors.reshape(-1, factors.shape[2])
    coeffs = exchange_sum(contract_rows(everyone, rows), n_aux)
    shares = lax.dot_general(
        rows, coeffs, (((1,), (1,)), ((), ())), preferred_element_type=jnp.float32
    )
    return lax.psum_scatter(
        shares.astype(jnp.bfloat16), "pair", scatter_dimension=0, tiled=True
    ).astype(jnp.float32)


def body(n_pair, n_aux, b_built, trial, energy_gap, block_live):
    blocks = trial.shape[0] // BLK
    own_blocks = lax.dynamic_slice_in_dim(block_live, lax.axis_index("aux") * blocks, blocks, 0)
    own_live = jnp.repeat(own_blocks, BLK)
    masked = trial * own_live.astype(jnp.bfloat16)[:, None]
    respond = along_line if n_pair == 4 else gathered
    response = respond(masked, b_built[0], n_aux)
    sigma_out = (
        energy_gap[:, None] * trial.astype(jnp.float32)
        + 2.0 * own_live.astype(jnp.float32)[:, None] * response
    )
    return sigma_out.astype(jnp.bfloat16)


def solution(mesh):
    n_pair, n_aux = mesh.shape["pair"], mesh.shape["aux"]
    return jax.shard_map(
        lambda *args: body(n_pair, n_aux, *args),
        mesh=mesh,
        in_specs=(
            P(("traj", "aux"), None, None, "pair"),
            P(("traj", "pair", "aux"), "root"),
            P(("traj", "pair", "aux")),
            P(("traj", "pair")),
        ),
        out_specs=P(("traj", "pair", "aux"), "root"),
        check_vma=False,
    )
```

```python
import functools

import jax
import jax.numpy as jnp
from jax import lax
from jax.experimental import pallas as pl
from jax.experimental.pallas import tpu as pltpu
from jax.sharding import PartitionSpec as P

BLK = 128
V_PARTS = 2

SMEM = pl.BlockSpec(memory_space=pltpu.SMEM)
VMEM = pl.BlockSpec(memory_space=pltpu.VMEM)
ANY = pl.BlockSpec(memory_space=pl.ANY)


def contract_rows(left, right):
    return lax.dot_general(
        left, right, (((0,), (0,)), ((), ())), preferred_element_type=jnp.float32
    )


def exchange_sum(partial, n_aux):
    sent = partial.astype(jnp.bfloat16)
    if n_aux == 1:
        return sent
    if n_aux == 2:
        other = lax.ppermute(sent, "aux", [(0, 1), (1, 0)])
        return (partial + other.astype(jnp.float32)).astype(jnp.bfloat16)
    return lax.psum(sent, "aux")


def block_rows(block):
    return pl.ds(pl.multiple_of(block * BLK, BLK), BLK)


def pack_trial_kernel(live_ref, trial_ref, *out_refs):
    width = out_refs[0].shape[1]
    for out in out_refs:
        out[...] = jnp.zeros_like(out)
    slot = jnp.int32(0)
    for block in range(trial_ref.shape[0] // BLK):
        here = live_ref[0, block]

        @pl.when(here > 0)
        def _(slot=slot, block=block):
            for part, out in enumerate(out_refs):
                out[block_rows(slot), :] = trial_ref[
                    pl.ds(block * BLK, BLK), pl.ds(part * width, width)
                ]

        slot = slot + here


def pack_factors_kernel(slots, live_ref, me_ref, factors_ref, out_ref, index_ref, sems):
    pairs, blocks = live_ref.shape
    copies = []
    for flip in range(pairs):
        for slot in range(blocks):
            index_ref[flip, slot] = 0
        at = jnp.int32(0)
        for block in range(blocks):
            index_ref[flip, at] = block
            at = at + live_ref[flip, block]
        for slot in range(slots):
            copies.append(
                pltpu.make_async_copy(
                    factors_ref.at[me_ref[0] ^ flip, block_rows(index_ref[flip, slot]), :],
                    out_ref.at[flip, pl.ds(slot * BLK, BLK), :],
                    sems.at[flip, slot],
                )
            )
            copies[-1].start()
    for copy in copies:
        copy.wait()


def unpack_kernel(live_ref, base_ref, own_ref, near_ref, inner_ref, far_ref, before_ref, out_ref):
    del before_ref
    slot = jnp.int32(0)
    for block in range(out_ref.shape[0] // BLK):
        rows = pl.ds(block * BLK, BLK)
        here = live_ref[0, block]

        @pl.when(here > 0)
        def _(slot=slot, rows=rows):
            at = block_rows(slot)
            response = own_ref[at, :]
            for ref in (near_ref, inner_ref, far_ref):
                response = response + ref[at, :].astype(jnp.float32)
            out_ref[rows, :] = (base_ref[rows, :] + 2.0 * response).astype(out_ref.dtype)

        @pl.when(here == 0)
        def _(rows=rows):
            out_ref[rows, :] = base_ref[rows, :].astype(out_ref.dtype)

        slot = slot + here


def along_line(slots, n_aux, live, trial, factors, base):
    me = lax.axis_index("pair")
    middle = (me == 1) | (me == 2)
    rows, vecs = trial.shape
    width = vecs // V_PARTS
    aux_here = factors.shape[2]
    near = [(z, z ^ 1) for z in range(4)]
    far = [(z, z ^ 2) for z in range(4)]
    inner = [(1, 2), (2, 1)]
    outward = [(2, 3), (1, 0)]
    inward = [(3, 2), (0, 1)]

    owns = pl.pallas_call(
        pack_trial_kernel,
        out_shape=[jax.ShapeDtypeStruct((slots * BLK, width), trial.dtype)] * V_PARTS,
        in_specs=[SMEM, VMEM],
        out_specs=[VMEM] * V_PARTS,
        name="pack_trial",
    )(live, trial)
    packed = pl.pallas_call(
        functools.partial(pack_factors_kernel, slots),
        out_shape=jax.ShapeDtypeStruct((4, slots * BLK, aux_here), factors.dtype),
        in_specs=[SMEM, SMEM, ANY],
        out_specs=ANY,
        scratch_shapes=[
            pltpu.SMEM((4, rows // BLK), jnp.int32),
            pltpu.SemaphoreType.DMA((4, slots)),
        ],
        name="pack_factors",
    )(live, me.astype(jnp.int32).reshape(1), factors)

    sigma = None
    for part, own in enumerate(owns):
        from_far = lax.ppermute(own, "pair", far)
        from_near = lax.ppermute(own, "pair", near)
        from_inner = lax.ppermute(own, "pair", inner)
        from_outer = lax.ppermute(from_far, "pair", outward)
        opposite = jnp.where(middle, from_inner, from_outer)
        partial = contract_rows(own, packed[0])
        partial = partial + contract_rows(from_near, packed[1])
        partial = partial + contract_rows(from_far, packed[2])
        partial = partial + contract_rows(opposite, packed[3])
        coeffs = exchange_sum(partial, n_aux)

        def share(flip):
            return lax.dot_general(
                packed[flip], coeffs, (((1,), (1,)), ((), ())), preferred_element_type=jnp.float32
            )

        share_3 = share(3).astype(jnp.bfloat16)
        got_outer = lax.ppermute(share_3, "pair", inward)
        got_inner = lax.ppermute(share_3, "pair", inner)
        got_near = lax.ppermute(share(1).astype(jnp.bfloat16), "pair", near)
        onward = share(2) + got_outer.astype(jnp.float32)
        got_far = lax.ppermute(onward.astype(jnp.bfloat16), "pair", far)
        half = pl.BlockSpec((rows, width), lambda _, part=part: (0, part))
        whole = [pl.BlockSpec((slots * BLK, width), lambda _: (0, 0))] * 4
        first = sigma is None
        sigma = pl.pallas_call(
            unpack_kernel if not first else lambda *refs: unpack_kernel(*refs[:-1], None, refs[-1]),
            out_shape=jax.ShapeDtypeStruct((rows, vecs), trial.dtype),
            grid=(1,),
            in_specs=[SMEM, half] + whole + ([] if first else [ANY]),
            out_specs=half,
            input_output_aliases={} if first else {6: 0},
            name="unpack",
        )(live, base, share(0), got_near, got_inner, got_far, *([] if first else [sigma]))
    return sigma


def gathered(masked, factors, n_aux):
    everyone = lax.all_gather(masked, "pair", axis=0, tiled=True)
    rows = factors.reshape(-1, factors.shape[2])
    coeffs = exchange_sum(contract_rows(everyone, rows), n_aux)
    shares = lax.dot_general(
        rows, coeffs, (((1,), (1,)), ((), ())), preferred_element_type=jnp.float32
    )
    return lax.psum_scatter(
        shares.astype(jnp.bfloat16), "pair", scatter_dimension=0, tiled=True
    ).astype(jnp.float32)


def body(n_traj, n_pair, n_aux, b_built, trial, energy_gap, block_live):
    blocks = trial.shape[0] // BLK
    aux = lax.axis_index("aux")
    base = energy_gap[:, None] * trial.astype(jnp.float32)
    if n_pair == 4:
        groups = n_traj * n_pair
        sent = jnp.broadcast_to(block_live[None], (groups, block_live.shape[0]))
        everyone = lax.all_to_all(sent, ("traj", "pair"), 0, 0, tiled=True)
        counts = everyone.reshape(groups, n_aux, blocks).sum(axis=2)
        least = (blocks * 5) // 8
        which = jnp.clip(jnp.max(counts) - least, 0, blocks - least)
        me = lax.axis_index("pair")
        order = lax.axis_index("traj") * n_pair + (me ^ jnp.arange(n_pair))
        columns = aux * blocks + jnp.arange(blocks)
        live = everyone[order[:, None], columns[None, :]]
        return lax.switch(
            which,
            [functools.partial(along_line, slots, n_aux) for slots in range(least, blocks + 1)],
            live,
            trial,
            b_built[0],
            base,
        )
    own_blocks = lax.dynamic_slice_in_dim(block_live, aux * blocks, blocks, 0)
    own_live = jnp.repeat(own_blocks, BLK)
    masked = trial * own_live.astype(jnp.bfloat16)[:, None]
    response = gathered(masked, b_built[0], n_aux)
    return (base + 2.0 * own_live.astype(jnp.float32)[:, None] * response).astype(jnp.bfloat16)


def solution(mesh):
    sizes = [mesh.shape[axis] for axis in ("traj", "pair", "aux")]
    return jax.shard_map(
        functools.partial(body, *sizes),
        mesh=mesh,
        in_specs=(
            P(("traj", "aux"), None, None, "pair"),
            P(("traj", "pair", "aux"), "root"),
            P(("traj", "pair", "aux")),
            P(("traj", "pair")),
        ),
        out_specs=P(("traj", "pair", "aux"), "root"),
        check_vma=False,
    )
```

```python
import functools

import jax
import jax.numpy as jnp
from jax import lax
from jax.experimental import pallas as pl
from jax.experimental.pallas import tpu as pltpu
from jax.sharding import PartitionSpec as P

BLK = 128
V_PARTS = 2

SMEM = pl.BlockSpec(memory_space=pltpu.SMEM)
VMEM = pl.BlockSpec(memory_space=pltpu.VMEM)
ANY = pl.BlockSpec(memory_space=pl.ANY)


def contract_rows(left, right):
    return lax.dot_general(
        left, right, (((0,), (0,)), ((), ())), preferred_element_type=jnp.float32
    )


def exchange_sum(partial, n_aux):
    sent = partial.astype(jnp.bfloat16)
    if n_aux == 1:
        return sent
    if n_aux == 2:
        other = lax.ppermute(sent, "aux", [(0, 1), (1, 0)])
        return (partial + other.astype(jnp.float32)).astype(jnp.bfloat16)
    return lax.psum(sent, "aux")


def block_rows(block):
    return pl.ds(pl.multiple_of(block * BLK, BLK), BLK)


def plan_kernel(least, aux_ref, own_ref, near_ref, far_ref, opposite_ref, live_ref, which_ref):
    blocks = live_ref.shape[1]
    most = jnp.int32(0)
    for flip, ref in enumerate((own_ref, near_ref, far_ref, opposite_ref)):
        for group in range(ref.shape[0] // blocks):
            count = ref[group * blocks]
            for block in range(1, blocks):
                count = count + ref[group * blocks + block]
            most = jnp.maximum(most, count)
        for block in range(blocks):
            live_ref[flip, block] = ref[aux_ref[0] * blocks + block]
    which_ref[0] = jnp.clip(most - least, 0, blocks - least)


def pack_trial_kernel(live_ref, trial_ref, *out_refs):
    width = out_refs[0].shape[1]
    for out in out_refs:
        out[...] = jnp.zeros_like(out)
    slot = jnp.int32(0)
    for block in range(trial_ref.shape[0] // BLK):
        here = live_ref[0, block]

        @pl.when(here > 0)
        def _(slot=slot, block=block):
            for part, out in enumerate(out_refs):
                out[block_rows(slot), :] = trial_ref[
                    pl.ds(block * BLK, BLK), pl.ds(part * width, width)
                ]

        slot = slot + here


def pack_factors_kernel(slots, live_ref, me_ref, factors_ref, out_ref, index_ref, sems):
    pairs, blocks = live_ref.shape
    copies = []
    for flip in range(pairs):
        for slot in range(blocks):
            index_ref[flip, slot] = 0
        at = jnp.int32(0)
        for block in range(blocks):
            index_ref[flip, at] = block
            at = at + live_ref[flip, block]
        for slot in range(slots):
            copies.append(
                pltpu.make_async_copy(
                    factors_ref.at[me_ref[0] ^ flip, block_rows(index_ref[flip, slot]), :],
                    out_ref.at[flip, pl.ds(slot * BLK, BLK), :],
                    sems.at[flip, slot],
                )
            )
            copies[-1].start()
    for copy in copies:
        copy.wait()


def unpack_kernel(live_ref, gap_ref, trial_ref, own_ref, near_ref, inner_ref, far_ref, before_ref, out_ref):
    del before_ref
    width = out_ref.shape[1]
    slot = jnp.int32(0)
    for block in range(out_ref.shape[0] // BLK):
        rows = pl.ds(block * BLK, BLK)
        here = live_ref[0, block]
        gap = jnp.transpose(jnp.broadcast_to(gap_ref[pl.ds(block, 1), :], (width, BLK)))
        base = gap * trial_ref[rows, :].astype(jnp.float32)

        @pl.when(here > 0)
        def _(slot=slot, rows=rows, base=base):
            at = block_rows(slot)
            response = own_ref[at, :]
            for ref in (near_ref, inner_ref, far_ref):
                response = response + ref[at, :].astype(jnp.float32)
            out_ref[rows, :] = (base + 2.0 * response).astype(out_ref.dtype)

        @pl.when(here == 0)
        def _(rows=rows, base=base):
            out_ref[rows, :] = base.astype(out_ref.dtype)

        slot = slot + here


def along_line(slots, n_aux, live, trial, factors, gap):
    me = lax.axis_index("pair")
    middle = (me == 1) | (me == 2)
    rows, vecs = trial.shape
    width = vecs // V_PARTS
    aux_here = factors.shape[2]
    near = [(z, z ^ 1) for z in range(4)]
    far = [(z, z ^ 2) for z in range(4)]
    inner = [(1, 2), (2, 1)]
    outward = [(2, 3), (1, 0)]
    inward = [(3, 2), (0, 1)]

    owns = pl.pallas_call(
        pack_trial_kernel,
        out_shape=[jax.ShapeDtypeStruct((slots * BLK, width), trial.dtype)] * V_PARTS,
        in_specs=[SMEM, VMEM],
        out_specs=[VMEM] * V_PARTS,
        name="pack_trial",
    )(live, trial)
    packed = pl.pallas_call(
        functools.partial(pack_factors_kernel, slots),
        out_shape=jax.ShapeDtypeStruct((4, slots * BLK, aux_here), factors.dtype),
        in_specs=[SMEM, SMEM, ANY],
        out_specs=VMEM,
        scratch_shapes=[
            pltpu.SMEM((4, rows // BLK), jnp.int32),
            pltpu.SemaphoreType.DMA((4, slots)),
        ],
        name="pack_factors",
    )(live, me.astype(jnp.int32).reshape(1), factors)

    sigma = None
    for part, own in enumerate(owns):
        from_far = lax.ppermute(own, "pair", far)
        from_near = lax.ppermute(own, "pair", near)
        from_inner = lax.ppermute(own, "pair", inner)
        from_outer = lax.ppermute(from_far, "pair", outward)
        opposite = jnp.where(middle, from_inner, from_outer)
        partial = contract_rows(own, packed[0])
        partial = partial + contract_rows(from_near, packed[1])
        partial = partial + contract_rows(from_far, packed[2])
        partial = partial + contract_rows(opposite, packed[3])
        coeffs = exchange_sum(partial, n_aux)

        def share(flip):
            return lax.dot_general(
                packed[flip], coeffs, (((1,), (1,)), ((), ())), preferred_element_type=jnp.float32
            )

        share_3 = share(3).astype(jnp.bfloat16)
        got_outer = lax.ppermute(share_3, "pair", inward)
        got_inner = lax.ppermute(share_3, "pair", inner)
        got_near = lax.ppermute(share(1).astype(jnp.bfloat16), "pair", near)
        onward = share(2) + got_outer.astype(jnp.float32)
        got_far = lax.ppermute(onward.astype(jnp.bfloat16), "pair", far)
        half = pl.BlockSpec((rows, width), lambda _, part=part: (0, part))
        whole = [pl.BlockSpec((slots * BLK, width), lambda _: (0, 0))] * 4
        first = sigma is None
        sigma = pl.pallas_call(
            unpack_kernel if not first else lambda *refs: unpack_kernel(*refs[:-1], None, refs[-1]),
            out_shape=jax.ShapeDtypeStruct((rows, vecs), trial.dtype),
            grid=(1,),
            in_specs=[SMEM, VMEM, half] + whole + ([] if first else [ANY]),
            out_specs=half,
            input_output_aliases={} if first else {7: 0},
            name="unpack",
        )(live, gap, trial, share(0), got_near, got_inner, got_far, *([] if first else [sigma]))
    return sigma


def gathered(masked, factors, n_aux):
    everyone = lax.all_gather(masked, "pair", axis=0, tiled=True)
    rows = factors.reshape(-1, factors.shape[2])
    coeffs = exchange_sum(contract_rows(everyone, rows), n_aux)
    shares = lax.dot_general(
        rows, coeffs, (((1,), (1,)), ((), ())), preferred_element_type=jnp.float32
    )
    return lax.psum_scatter(
        shares.astype(jnp.bfloat16), "pair", scatter_dimension=0, tiled=True
    ).astype(jnp.float32)


def body(n_pair, n_aux, b_built, trial, energy_gap, block_live):
    blocks = trial.shape[0] // BLK
    aux = lax.axis_index("aux")
    if n_pair == 4:
        least = (blocks * 5) // 8
        flags = [block_live] + [
            lax.ppermute(block_live, "pair", [(z, z ^ flip) for z in range(n_pair)])
            for flip in range(1, n_pair)
        ]
        live, which = pl.pallas_call(
            functools.partial(plan_kernel, least),
            out_shape=[
                jax.ShapeDtypeStruct((n_pair, blocks), jnp.int32),
                jax.ShapeDtypeStruct((1,), jnp.int32),
            ],
            in_specs=[SMEM] * 5,
            out_specs=[SMEM] * 2,
            name="plan",
        )(aux.astype(jnp.int32).reshape(1), *flags)
        return lax.switch(
            which[0],
            [functools.partial(along_line, slots, n_aux) for slots in range(least, blocks + 1)],
            live,
            trial,
            b_built[0],
            energy_gap.reshape(blocks, BLK),
        )
    own_blocks = lax.dynamic_slice_in_dim(block_live, aux * blocks, blocks, 0)
    own_live = jnp.repeat(own_blocks, BLK)
    masked = trial * own_live.astype(jnp.bfloat16)[:, None]
    response = gathered(masked, b_built[0], n_aux)
    base = energy_gap[:, None] * trial.astype(jnp.float32)
    return (base + 2.0 * own_live.astype(jnp.float32)[:, None] * response).astype(jnp.bfloat16)


def solution(mesh):
    sizes = [mesh.shape[axis] for axis in ("pair", "aux")]
    return jax.shard_map(
        functools.partial(body, *sizes),
        mesh=mesh,
        in_specs=(
            P(("traj", "aux"), None, None, "pair"),
            P(("traj", "pair", "aux"), "root"),
            P(("traj", "pair", "aux")),
            P(("traj", "pair")),
        ),
        out_specs=P(("traj", "pair", "aux"), "root"),
        check_vma=False,
    )
```

```python
import functools

import jax
import jax.numpy as jnp
from jax import lax
from jax.experimental import pallas as pl
from jax.experimental.pallas import tpu as pltpu
from jax.sharding import PartitionSpec as P

BLK = 128
V_PARTS = 2

SMEM = pl.BlockSpec(memory_space=pltpu.SMEM)
VMEM = pl.BlockSpec(memory_space=pltpu.VMEM)
ANY = pl.BlockSpec(memory_space=pl.ANY)


def contract_rows(left, right):
    return lax.dot_general(
        left, right, (((0,), (0,)), ((), ())), preferred_element_type=jnp.float32
    )


def exchange_sum(partial, n_aux):
    sent = partial.astype(jnp.bfloat16)
    if n_aux == 1:
        return sent
    if n_aux == 2:
        other = lax.ppermute(sent, "aux", [(0, 1), (1, 0)])
        return (partial + other.astype(jnp.float32)).astype(jnp.bfloat16)
    return lax.psum(sent, "aux")


def block_rows(block):
    return pl.ds(pl.multiple_of(block * BLK, BLK), BLK)


def plan_kernel(least, aux_ref, own_ref, near_ref, far_ref, opposite_ref, live_ref, which_ref):
    blocks = live_ref.shape[1]
    most = jnp.int32(0)
    for flip, ref in enumerate((own_ref, near_ref, far_ref, opposite_ref)):
        for group in range(ref.shape[0] // blocks):
            count = ref[group * blocks]
            for block in range(1, blocks):
                count = count + ref[group * blocks + block]
            most = jnp.maximum(most, count)
        for block in range(blocks):
            live_ref[flip, block] = ref[aux_ref[0] * blocks + block]
    which_ref[0] = jnp.clip(most - least, 0, blocks - least)


def pack_trial_kernel(aux_ref, live_ref, trial_ref, *out_refs):
    width = out_refs[0].shape[1]
    for out in out_refs:
        out[...] = jnp.zeros_like(out)
    slot = jnp.int32(0)
    blocks = trial_ref.shape[0] // BLK
    for block in range(blocks):
        here = live_ref[aux_ref[0] * blocks + block]

        @pl.when(here > 0)
        def _(slot=slot, block=block):
            for part, out in enumerate(out_refs):
                out[block_rows(slot), :] = trial_ref[
                    pl.ds(block * BLK, BLK), pl.ds(part * width, width)
                ]

        slot = slot + here


def pack_factors_kernel(slots, live_ref, me_ref, factors_ref, out_ref, index_ref, sems):
    pairs, blocks = live_ref.shape
    copies = []
    for flip in range(pairs):
        for slot in range(blocks):
            index_ref[flip, slot] = 0
        at = jnp.int32(0)
        for block in range(blocks):
            index_ref[flip, at] = block
            at = at + live_ref[flip, block]
        for slot in range(slots):
            copies.append(
                pltpu.make_async_copy(
                    factors_ref.at[me_ref[0] ^ flip, block_rows(index_ref[flip, slot]), :],
                    out_ref.at[flip, pl.ds(slot * BLK, BLK), :],
                    sems.at[flip, slot],
                )
            )
            copies[-1].start()
    for copy in copies:
        copy.wait()


def settle_kernel(live_ref, gap_ref, trial_ref, own_ref, near_ref, inner_ref, out_ref):
    width = out_ref.shape[1]
    slot = jnp.int32(0)
    for block in range(out_ref.shape[0] // BLK):
        rows = pl.ds(block * BLK, BLK)
        here = live_ref[0, block]
        gap = jnp.transpose(jnp.broadcast_to(gap_ref[pl.ds(block, 1), :], (width, BLK)))
        base = gap * trial_ref[rows, :].astype(jnp.float32)

        @pl.when(here > 0)
        def _(slot=slot, rows=rows, base=base):
            at = block_rows(slot)
            response = own_ref[at, :]
            for ref in (near_ref, inner_ref):
                response = response + ref[at, :].astype(jnp.float32)
            out_ref[rows, :] = base + 2.0 * response

        @pl.when(here == 0)
        def _(rows=rows, base=base):
            out_ref[rows, :] = base

        slot = slot + here


def finish_kernel(live_ref, settled_ref, far_ref, *refs):
    out_ref = refs[-1]
    slot = jnp.int32(0)
    for block in range(out_ref.shape[0] // BLK):
        rows = pl.ds(block * BLK, BLK)
        here = live_ref[0, block]

        @pl.when(here > 0)
        def _(slot=slot, rows=rows):
            far = far_ref[block_rows(slot), :].astype(jnp.float32)
            out_ref[rows, :] = (settled_ref[rows, :] + 2.0 * far).astype(out_ref.dtype)

        @pl.when(here == 0)
        def _(rows=rows):
            out_ref[rows, :] = settled_ref[rows, :].astype(out_ref.dtype)

        slot = slot + here


NEAR = [(z, z ^ 1) for z in range(4)]
FAR = [(z, z ^ 2) for z in range(4)]
INNER = [(1, 2), (2, 1)]
OUTWARD = [(2, 3), (1, 0)]
INWARD = [(3, 2), (0, 1)]


def after(value, *others):
    return lax.optimization_barrier((value, *others))[0]


def along_line(slots, n_aux, live, trial, gap, packed, owns, first_got):
    me = lax.axis_index("pair")
    middle = (me == 1) | (me == 2)
    rows, vecs = trial.shape
    width = vecs // V_PARTS
    held = slots * BLK
    factors = [packed[flip, :held] for flip in range(4)]

    sigma = None
    sums = []
    for part in range(V_PARTS):
        if part == 0:
            own, from_far, from_near, from_inner = (got[:held] for got in (owns[0], *first_got))
        else:
            own = owns[part][:held]
            from_far = lax.ppermute(own, "pair", FAR)
            from_near = lax.ppermute(own, "pair", NEAR)
            from_inner = lax.ppermute(own, "pair", INNER)
            from_far = after(from_far, sums[-1])
        from_outer = lax.ppermute(from_far, "pair", OUTWARD)
        partial = contract_rows(own, factors[0])
        partial = partial + contract_rows(from_near, factors[1])
        partial = partial + contract_rows(from_far, factors[2])
        opposite = jnp.where(middle, from_inner, from_outer)
        partial = partial + contract_rows(opposite, factors[3])
        sums.append(partial)

    for part, partial in enumerate(sums):
        coeffs = exchange_sum(partial, n_aux)

        def share(flip):
            return lax.dot_general(
                factors[flip], coeffs, (((1,), (1,)), ((), ())), preferred_element_type=jnp.float32
            )

        share_3 = share(3).astype(jnp.bfloat16)
        got_outer = lax.ppermute(share_3, "pair", INWARD)
        got_inner = lax.ppermute(share_3, "pair", INNER)
        got_near = lax.ppermute(share(1).astype(jnp.bfloat16), "pair", NEAR)
        onward = share(2) + got_outer.astype(jnp.float32)
        got_far = lax.ppermute(onward.astype(jnp.bfloat16), "pair", FAR)
        half = pl.BlockSpec((rows, width), lambda _, part=part: (0, part))
        settled = pl.pallas_call(
            settle_kernel,
            out_shape=jax.ShapeDtypeStruct((rows, width), jnp.float32),
            grid=(1,),
            in_specs=[SMEM, VMEM, half, VMEM, VMEM, VMEM],
            out_specs=VMEM,
            name="settle",
        )(live, gap, trial, share(0), got_near, got_inner)
        first = sigma is None
        sigma = pl.pallas_call(
            finish_kernel,
            out_shape=jax.ShapeDtypeStruct((rows, vecs), trial.dtype),
            grid=(1,),
            in_specs=[SMEM, VMEM, VMEM] + ([] if first else [ANY]),
            out_specs=half,
            input_output_aliases={} if first else {3: 0},
            name="finish",
        )(live, settled, got_far, *([] if first else [sigma]))
    return sigma


def on_four(n_aux, factors, trial, energy_gap, block_live):
    rows, vecs = trial.shape
    blocks = rows // BLK
    least = (blocks * 5) // 8
    aux = lax.axis_index("aux").astype(jnp.int32).reshape(1)
    me = lax.axis_index("pair").astype(jnp.int32).reshape(1)
    flags = [block_live] + [
        lax.ppermute(block_live, "pair", [(z, z ^ flip) for z in range(4)]) for flip in range(1, 4)
    ]
    owns = pl.pallas_call(
        pack_trial_kernel,
        out_shape=[jax.ShapeDtypeStruct((rows, vecs // V_PARTS), trial.dtype)] * V_PARTS,
        in_specs=[SMEM, SMEM, VMEM],
        out_specs=[VMEM] * V_PARTS,
        name="pack_trial",
    )(aux, block_live, trial)
    first = after(owns[0], *flags[1:])
    first_got = [lax.ppermute(first, "pair", pairs) for pairs in (FAR, NEAR, INNER)]
    live, which = pl.pallas_call(
        functools.partial(plan_kernel, least),
        out_shape=[
            jax.ShapeDtypeStruct((4, blocks), jnp.int32),
            jax.ShapeDtypeStruct((1,), jnp.int32),
        ],
        in_specs=[SMEM] * 5,
        out_specs=[SMEM] * 2,
        name="plan",
    )(aux, *flags)
    packed = pl.pallas_call(
        functools.partial(pack_factors_kernel, blocks),
        out_shape=jax.ShapeDtypeStruct(factors.shape, factors.dtype),
        in_specs=[SMEM, SMEM, ANY],
        out_specs=VMEM,
        scratch_shapes=[
            pltpu.SMEM((4, blocks), jnp.int32),
            pltpu.SemaphoreType.DMA((4, blocks)),
        ],
        name="pack_factors",
    )(live, me, factors)
    return lax.switch(
        which[0],
        [functools.partial(along_line, slots, n_aux) for slots in range(least, blocks + 1)],
        live,
        trial,
        energy_gap.reshape(blocks, BLK),
        packed,
        owns,
        first_got,
    )


def gathered(masked, factors, n_aux):
    everyone = lax.all_gather(masked, "pair", axis=0, tiled=True)
    rows = factors.reshape(-1, factors.shape[2])
    coeffs = exchange_sum(contract_rows(everyone, rows), n_aux)
    shares = lax.dot_general(
        rows, coeffs, (((1,), (1,)), ((), ())), preferred_element_type=jnp.float32
    )
    return lax.psum_scatter(
        shares.astype(jnp.bfloat16), "pair", scatter_dimension=0, tiled=True
    ).astype(jnp.float32)


def body(n_pair, n_aux, b_built, trial, energy_gap, block_live):
    blocks = trial.shape[0] // BLK
    aux = lax.axis_index("aux")
    if n_pair == 4:
        return on_four(n_aux, b_built[0], trial, energy_gap, block_live)
    own_blocks = lax.dynamic_slice_in_dim(block_live, aux * blocks, blocks, 0)
    own_live = jnp.repeat(own_blocks, BLK)
    masked = trial * own_live.astype(jnp.bfloat16)[:, None]
    response = gathered(masked, b_built[0], n_aux)
    base = energy_gap[:, None] * trial.astype(jnp.float32)
    return (base + 2.0 * own_live.astype(jnp.float32)[:, None] * response).astype(jnp.bfloat16)


def solution(mesh):
    sizes = [mesh.shape[axis] for axis in ("pair", "aux")]
    return jax.shard_map(
        functools.partial(body, *sizes),
        mesh=mesh,
        in_specs=(
            P(("traj", "aux"), None, None, "pair"),
            P(("traj", "pair", "aux"), "root"),
            P(("traj", "pair", "aux")),
            P(("traj", "pair")),
        ),
        out_specs=P(("traj", "pair", "aux"), "root"),
        check_vma=False,
    )
```

```python
import functools

import jax
import jax.numpy as jnp
from jax import lax
from jax.experimental import pallas as pl
from jax.experimental.pallas import tpu as pltpu
from jax.sharding import PartitionSpec as P

BLK = 128
V_PARTS = 2

SMEM = pl.BlockSpec(memory_space=pltpu.SMEM)
VMEM = pl.BlockSpec(memory_space=pltpu.VMEM)
ANY = pl.BlockSpec(memory_space=pl.ANY)


def contract_rows(left, right):
    return lax.dot_general(
        left, right, (((0,), (0,)), ((), ())), preferred_element_type=jnp.float32
    )


def exchange_sum(partial, n_aux):
    sent = partial.astype(jnp.bfloat16)
    if n_aux == 1:
        return sent
    if n_aux == 2:
        other = lax.ppermute(sent, "aux", [(0, 1), (1, 0)])
        return (partial + other.astype(jnp.float32)).astype(jnp.bfloat16)
    return lax.psum(sent, "aux")


def block_rows(block):
    return pl.ds(pl.multiple_of(block * BLK, BLK), BLK)


def plan_kernel(classes, at_ref, own_ref, near_ref, far_ref, opposite_ref, live_ref, pairs_ref, which_ref):
    blocks = live_ref.shape[1]
    me = at_ref[0]
    end = (me == 0) | (me == 3)

    def most(ref):
        top = jnp.int32(0)
        for group in range(ref.shape[0] // blocks):
            count = ref[group * blocks]
            for block in range(1, blocks):
                count = count + ref[group * blocks + block]
            top = jnp.maximum(top, count)
        return top

    alike = jnp.maximum(most(own_ref), most(opposite_ref))
    unlike = jnp.maximum(most(near_ref), most(far_ref))
    at_ends = jnp.where(end, alike, unlike)
    at_middles = jnp.where(end, unlike, alike)
    which = jnp.int32(len(classes) - 1)
    for at in range(len(classes) - 2, -1, -1):
        fits = (at_ends <= classes[at][0]) & (at_middles <= classes[at][1])
        which = jnp.where(fits, at, which)
    which_ref[0] = which
    rows = ((own_ref, 0, far_ref, 2), (far_ref, 2, own_ref, 0), (opposite_ref, 3, near_ref, 1), (near_ref, 1, opposite_ref, 3))
    for row, (if_end, end_flip, if_middle, middle_flip) in enumerate(rows):
        pairs_ref[row] = me ^ jnp.where(end, end_flip, middle_flip)
        for block in range(blocks):
            at = at_ref[1] * blocks + block
            live_ref[row, block] = jnp.where(end, if_end[at], if_middle[at])


def pack_trial_kernel(at_ref, live_ref, trial_ref, *out_refs):
    width = out_refs[0].shape[1]
    for out in out_refs:
        out[...] = jnp.zeros_like(out)
    slot = jnp.int32(0)
    blocks = trial_ref.shape[0] // BLK
    for block in range(blocks):
        here = live_ref[at_ref[1] * blocks + block]

        @pl.when(here > 0)
        def _(slot=slot, block=block):
            for part, out in enumerate(out_refs):
                out[block_rows(slot), :] = trial_ref[
                    pl.ds(block * BLK, BLK), pl.ds(part * width, width)
                ]

        slot = slot + here


def pack_factors_kernel(ends, middles, live_ref, pairs_ref, factors_ref, own_ref, near_ref, index_ref, sems):
    blocks = live_ref.shape[1]
    copies = []
    places = ((own_ref, 0, ends), (own_ref, ends, middles), (near_ref, 0, ends), (near_ref, ends, middles))
    for row, (out, start, slots) in enumerate(places):
        for slot in range(blocks):
            index_ref[row, slot] = 0
        at = jnp.int32(0)
        for block in range(blocks):
            index_ref[row, at] = block
            at = at + live_ref[row, block]
        for slot in range(slots):
            copies.append(
                pltpu.make_async_copy(
                    factors_ref.at[pairs_ref[row], block_rows(index_ref[row, slot]), :],
                    out.at[pl.ds((start + slot) * BLK, BLK), :],
                    sems.at[row, slot],
                )
            )
            copies[-1].start()
    for copy in copies:
        copy.wait()


def finish_kernel(ends, at_ref, live_ref, gap_ref, trial_ref, sum_ref, ends_ref, middles_ref, *refs):
    out_ref = refs[-1]
    width = out_ref.shape[1]
    end = (at_ref[0] == 0) | (at_ref[0] == 3)
    slot = jnp.int32(0)
    for block in range(out_ref.shape[0] // BLK):
        rows = pl.ds(block * BLK, BLK)
        here = jnp.where(end, live_ref[0, block], live_ref[1, block])
        gap = jnp.transpose(jnp.broadcast_to(gap_ref[pl.ds(block, 1), :], (width, BLK)))
        base = gap * trial_ref[rows, :].astype(jnp.float32)

        def put(rows, base, response):
            out_ref[rows, :] = (base + 2.0 * response).astype(out_ref.dtype)

        @pl.when((here > 0) & end)
        def _(slot=slot, rows=rows, base=base):
            at = block_rows(slot)
            put(rows, base, sum_ref[at, :] + ends_ref[at, :].astype(jnp.float32))

        @pl.when((here > 0) & jnp.logical_not(end))
        def _(slot=slot, rows=rows, base=base):
            last = middles_ref[block_rows(slot), :].astype(jnp.float32)
            put(rows, base, sum_ref[block_rows(ends + slot), :] + last)

        @pl.when(here == 0)
        def _(rows=rows, base=base):
            out_ref[rows, :] = base.astype(out_ref.dtype)

        slot = slot + here


NEAR = [(z, z ^ 1) for z in range(4)]
FAR = [(z, z ^ 2) for z in range(4)]
FROM_ENDS = [(0, 2), (3, 1)]
FROM_MIDDLES = [(1, 3), (2, 0)]


def room(mebibytes):
    return pltpu.CompilerParams(vmem_limit_bytes=mebibytes * 2**20)


def after(value, *others):
    return lax.optimization_barrier((value, *others))[0]


def along_line(ends, middles, n_aux, at, live, pairs, trial, gap, factors, owns, first_far):
    rows, vecs = trial.shape
    width = vecs // V_PARTS
    end = (at[0] == 0) | (at[0] == 3)
    e_rows, m_rows = ends * BLK, middles * BLK
    held = e_rows + m_rows

    def side(own, from_ends, from_middles):
        return jnp.concatenate(
            [
                jnp.where(end, own[:e_rows], from_ends[:e_rows]),
                jnp.where(end, from_middles[:m_rows], own[:m_rows]),
            ]
        )

    mine = [side(owns[0], first_far, first_far)]
    theirs = [lax.ppermute(mine[0], "pair", NEAR)]
    from_ends = lax.ppermute(owns[1][:e_rows], "pair", FROM_ENDS)
    from_middles = lax.ppermute(owns[1][:m_rows], "pair", FROM_MIDDLES)
    own_factors, near_factors = pl.pallas_call(
        functools.partial(pack_factors_kernel, ends, middles),
        out_shape=[jax.ShapeDtypeStruct((held, factors.shape[2]), factors.dtype)] * 2,
        in_specs=[SMEM, SMEM, ANY],
        out_specs=[VMEM, VMEM],
        scratch_shapes=[
            pltpu.SMEM((4, rows // BLK), jnp.int32),
            pltpu.SemaphoreType.DMA((4, max(ends, middles))),
        ],
        compiler_params=room(10),
        name="pack_factors",
    )(live, pairs, factors)
    mine.append(side(owns[1], from_ends, from_middles))
    theirs.append(lax.ppermute(mine[1], "pair", NEAR))

    sigma = None
    for part in range(V_PARTS):
        partial = contract_rows(mine[part], own_factors) + contract_rows(theirs[part], near_factors)
        coeffs = exchange_sum(partial, n_aux)

        def share(of):
            return lax.dot_general(
                of, coeffs, (((1,), (1,)), ((), ())), preferred_element_type=jnp.float32
            )

        got_near = lax.ppermute(share(near_factors).astype(jnp.bfloat16), "pair", NEAR)
        total = share(own_factors) + got_near.astype(jnp.float32)
        sent = total.astype(jnp.bfloat16)
        for_ends = lax.ppermute(sent[:e_rows], "pair", FROM_MIDDLES)
        for_middles = lax.ppermute(sent[e_rows:], "pair", FROM_ENDS)
        half = pl.BlockSpec((rows, width), lambda _, part=part: (0, part))
        first = sigma is None
        sigma = pl.pallas_call(
            functools.partial(finish_kernel, ends),
            out_shape=jax.ShapeDtypeStruct((rows, vecs), trial.dtype),
            grid=(1,),
            in_specs=[SMEM, SMEM, VMEM, half, VMEM, VMEM, VMEM] + ([] if first else [ANY]),
            out_specs=half,
            input_output_aliases={} if first else {7: 0},
            compiler_params=room(8),
            name="finish",
        )(at, live, gap, trial, total, for_ends, for_middles, *([] if first else [sigma]))
    return sigma


def on_four(n_aux, factors, trial, energy_gap, block_live):
    rows, vecs = trial.shape
    blocks = rows // BLK
    classes = [(3, 5), (5, 3), (3, 6), (6, 3), (4, 6), (6, 4), (4, 7), (7, 4)]
    classes = [pair for pair in classes if max(pair) <= blocks] + [(blocks, blocks)]
    at = jnp.stack([lax.axis_index("pair"), lax.axis_index("aux")]).astype(jnp.int32)
    flags = [block_live] + [
        lax.ppermute(block_live, "pair", [(z, z ^ flip) for z in range(4)]) for flip in range(1, 4)
    ]
    owns = pl.pallas_call(
        pack_trial_kernel,
        out_shape=[jax.ShapeDtypeStruct((rows, vecs // V_PARTS), trial.dtype)] * V_PARTS,
        in_specs=[SMEM, SMEM, VMEM],
        out_specs=[VMEM] * V_PARTS,
        compiler_params=room(4),
        name="pack_trial",
    )(at, block_live, trial)
    first_far = lax.ppermute(after(owns[0], *flags[1:]), "pair", FAR)
    live, pairs, which = pl.pallas_call(
        functools.partial(plan_kernel, classes),
        out_shape=[
            jax.ShapeDtypeStruct((4, blocks), jnp.int32),
            jax.ShapeDtypeStruct((4,), jnp.int32),
            jax.ShapeDtypeStruct((1,), jnp.int32),
        ],
        in_specs=[SMEM] * 5,
        out_specs=[SMEM] * 3,
        compiler_params=room(2),
        name="plan",
    )(at, *flags)
    return lax.switch(
        which[0],
        [functools.partial(along_line, *pair, n_aux) for pair in classes],
        at,
        live,
        pairs,
        trial,
        energy_gap.reshape(blocks, BLK),
        factors,
        owns,
        first_far,
    )


def gathered(masked, factors, n_aux):
    everyone = lax.all_gather(masked, "pair", axis=0, tiled=True)
    rows = factors.reshape(-1, factors.shape[2])
    coeffs = exchange_sum(contract_rows(everyone, rows), n_aux)
    shares = lax.dot_general(
        rows, coeffs, (((1,), (1,)), ((), ())), preferred_element_type=jnp.float32
    )
    return lax.psum_scatter(
        shares.astype(jnp.bfloat16), "pair", scatter_dimension=0, tiled=True
    ).astype(jnp.float32)


def body(n_pair, n_aux, b_built, trial, energy_gap, block_live):
    blocks = trial.shape[0] // BLK
    aux = lax.axis_index("aux")
    if n_pair == 4:
        return on_four(n_aux, b_built[0], trial, energy_gap, block_live)
    own_blocks = lax.dynamic_slice_in_dim(block_live, aux * blocks, blocks, 0)
    own_live = jnp.repeat(own_blocks, BLK)
    masked = trial * own_live.astype(jnp.bfloat16)[:, None]
    response = gathered(masked, b_built[0], n_aux)
    base = energy_gap[:, None] * trial.astype(jnp.float32)
    return (base + 2.0 * own_live.astype(jnp.float32)[:, None] * response).astype(jnp.bfloat16)


def solution(mesh):
    sizes = [mesh.shape[axis] for axis in ("pair", "aux")]
    return jax.shard_map(
        functools.partial(body, *sizes),
        mesh=mesh,
        in_specs=(
            P(("traj", "aux"), None, None, "pair"),
            P(("traj", "pair", "aux"), "root"),
            P(("traj", "pair", "aux")),
            P(("traj", "pair")),
        ),
        out_specs=P(("traj", "pair", "aux"), "root"),
        check_vma=False,
    )
```

```python
import functools

import jax
import jax.numpy as jnp
from jax import lax
from jax.experimental import pallas as pl
from jax.experimental.pallas import tpu as pltpu
from jax.sharding import PartitionSpec as P

BLK = 128
V_PARTS = 2

SMEM = pl.BlockSpec(memory_space=pltpu.SMEM)
VMEM = pl.BlockSpec(memory_space=pltpu.VMEM)
ANY = pl.BlockSpec(memory_space=pl.ANY)


def contract_rows(left, right):
    return lax.dot_general(
        left, right, (((0,), (0,)), ((), ())), preferred_element_type=jnp.float32
    )


def exchange_sum(partial, n_aux):
    sent = partial.astype(jnp.bfloat16)
    if n_aux == 1:
        return sent
    if n_aux == 2:
        other = lax.ppermute(sent, "aux", [(0, 1), (1, 0)])
        return (partial + other.astype(jnp.float32)).astype(jnp.bfloat16)
    return lax.psum(sent, "aux")


def block_rows(block):
    return pl.ds(pl.multiple_of(block * BLK, BLK), BLK)


def plan_kernel(classes, at_ref, own_ref, near_ref, far_ref, opposite_ref, live_ref, pairs_ref, which_ref, large_ref):
    blocks = live_ref.shape[1]
    me = at_ref[0]

    def most(ref):
        top = jnp.int32(0)
        for group in range(ref.shape[0] // blocks):
            count = ref[group * blocks]
            for block in range(1, blocks):
                count = count + ref[group * blocks + block]
            top = jnp.maximum(top, count)
        return top

    alike = jnp.maximum(most(own_ref), most(opposite_ref))
    unlike = jnp.maximum(most(near_ref), most(far_ref))
    end = (me == 0) | (me == 3)
    ends_large = jnp.where(end, alike, unlike) >= jnp.where(end, unlike, alike)
    large = end == ends_large
    large_ref[0] = large.astype(jnp.int32)
    top, other = jnp.maximum(alike, unlike), jnp.minimum(alike, unlike)
    which = jnp.int32(len(classes) - 1)
    for at in range(len(classes) - 2, -1, -1):
        which = jnp.where((top <= classes[at][0]) & (other <= classes[at][1]), at, which)
    which_ref[0] = which
    rows = (((own_ref, 0), (far_ref, 2)), ((far_ref, 2), (own_ref, 0)), ((opposite_ref, 3), (near_ref, 1)), ((near_ref, 1), (opposite_ref, 3)))
    for row, ((if_large, large_flip), (if_small, small_flip)) in enumerate(rows):
        pairs_ref[row] = me ^ jnp.where(large, large_flip, small_flip)
        for block in range(blocks):
            at = at_ref[1] * blocks + block
            live_ref[row, block] = jnp.where(large, if_large[at], if_small[at])


def pack_trial_kernel(at_ref, live_ref, trial_ref, *out_refs):
    width = out_refs[0].shape[1]
    for out in out_refs:
        out[...] = jnp.zeros_like(out)
    slot = jnp.int32(0)
    blocks = trial_ref.shape[0] // BLK
    for block in range(blocks):
        here = live_ref[at_ref[1] * blocks + block]

        @pl.when(here > 0)
        def _(slot=slot, block=block):
            for part, out in enumerate(out_refs):
                out[block_rows(slot), :] = trial_ref[
                    pl.ds(block * BLK, BLK), pl.ds(part * width, width)
                ]

        slot = slot + here


def pack_factors_kernel(most, rest, live_ref, pairs_ref, factors_ref, own_ref, near_ref, index_ref, sems):
    blocks = live_ref.shape[1]
    copies = []
    places = ((own_ref, 0, most), (own_ref, most, rest), (near_ref, 0, most), (near_ref, most, rest))
    for row, (out, start, slots) in enumerate(places):
        for slot in range(blocks):
            index_ref[row, slot] = 0
        at = jnp.int32(0)
        for block in range(blocks):
            index_ref[row, at] = block
            at = at + live_ref[row, block]
        for slot in range(slots):
            copies.append(
                pltpu.make_async_copy(
                    factors_ref.at[pairs_ref[row], block_rows(index_ref[row, slot]), :],
                    out.at[pl.ds((start + slot) * BLK, BLK), :],
                    sems.at[row, slot],
                )
            )
            copies[-1].start()
    for copy in copies:
        copy.wait()


def finish_kernel(most, large_ref, live_ref, gap_ref, trial_ref, sum_ref, far_ref, *refs):
    out_ref = refs[-1]
    width = out_ref.shape[1]
    large = large_ref[0]
    start = (1 - large) * most
    slot = jnp.int32(0)
    for block in range(out_ref.shape[0] // BLK):
        rows = pl.ds(block * BLK, BLK)
        here = jnp.where(large > 0, live_ref[0, block], live_ref[1, block])
        gap = jnp.transpose(jnp.broadcast_to(gap_ref[pl.ds(block, 1), :], (width, BLK)))
        base = gap * trial_ref[rows, :].astype(jnp.float32)

        @pl.when(here > 0)
        def _(slot=slot, rows=rows, base=base):
            response = sum_ref[block_rows(start + slot), :] + far_ref[block_rows(slot), :].astype(jnp.float32)
            out_ref[rows, :] = (base + 2.0 * response).astype(out_ref.dtype)

        @pl.when(here == 0)
        def _(rows=rows, base=base):
            out_ref[rows, :] = base.astype(out_ref.dtype)

        slot = slot + here


NEAR = [(z, z ^ 1) for z in range(4)]
FAR = [(z, z ^ 2) for z in range(4)]


def room(mebibytes):
    return pltpu.CompilerParams(vmem_limit_bytes=mebibytes * 2**20)


def after(value, *others):
    return lax.optimization_barrier((value, *others))[0]


def along_line(most, rest, n_aux, large, live, pairs, trial, gap, factors, owns, first_far):
    rows, vecs = trial.shape
    width = vecs // V_PARTS
    is_large = large[0] > 0
    cut = most * BLK
    held = cut + rest * BLK

    def side(own, far):
        return jnp.concatenate(
            [jnp.where(is_large, own[:cut], far[:cut]), jnp.where(is_large, far, own)[: held - cut]]
        )

    mine = [side(owns[0], first_far)]
    theirs = [lax.ppermute(mine[0], "pair", NEAR)]
    second_far = lax.ppermute(after(owns[1], mine[0])[:cut], "pair", FAR)
    own_factors, near_factors = pl.pallas_call(
        functools.partial(pack_factors_kernel, most, rest),
        out_shape=[jax.ShapeDtypeStruct((held, factors.shape[2]), factors.dtype)] * 2,
        in_specs=[SMEM, SMEM, ANY],
        out_specs=[VMEM, VMEM],
        scratch_shapes=[
            pltpu.SMEM((4, rows // BLK), jnp.int32),
            pltpu.SemaphoreType.DMA((4, most)),
        ],
        compiler_params=room(10),
        name="pack_factors",
    )(live, pairs, factors)
    mine.append(side(owns[1][:cut], second_far))
    theirs.append(lax.ppermute(mine[1], "pair", NEAR))

    sigma = for_near = None
    for part in range(V_PARTS):
        got = theirs[part] if for_near is None else after(theirs[part], for_near)
        partial = contract_rows(mine[part], own_factors) + contract_rows(got, near_factors)
        coeffs = exchange_sum(partial, n_aux)

        def share(of):
            return lax.dot_general(
                of, coeffs, (((1,), (1,)), ((), ())), preferred_element_type=jnp.float32
            )

        for_near = share(near_factors).astype(jnp.bfloat16)
        got_near = lax.ppermute(for_near, "pair", NEAR)
        total = share(own_factors) + got_near.astype(jnp.float32)
        for_small = total[cut:]
        if most > rest:
            for_small = jnp.pad(for_small, ((0, 2 * cut - held), (0, 0)))
        for_far = jnp.where(is_large, for_small, total[:cut]).astype(jnp.bfloat16)
        got_far = lax.ppermute(for_far, "pair", FAR)
        half = pl.BlockSpec((rows, width), lambda _, part=part: (0, part))
        first = sigma is None
        sigma = pl.pallas_call(
            functools.partial(finish_kernel, most),
            out_shape=jax.ShapeDtypeStruct((rows, vecs), trial.dtype),
            grid=(1,),
            in_specs=[SMEM, SMEM, VMEM, half, VMEM, VMEM] + ([] if first else [ANY]),
            out_specs=half,
            input_output_aliases={} if first else {6: 0},
            compiler_params=room(8),
            name="finish",
        )(large, live, gap, trial, total, got_far, *([] if first else [sigma]))
    return sigma


def on_four(n_aux, factors, trial, energy_gap, block_live):
    rows, vecs = trial.shape
    blocks = rows // BLK
    classes = [pair for pair in ((6, 3), (6, 4), (7, 4)) if max(pair) < blocks] + [(blocks, blocks)]
    at = jnp.stack([lax.axis_index("pair"), lax.axis_index("aux")]).astype(jnp.int32)
    flags = [block_live] + [
        lax.ppermute(block_live, "pair", [(z, z ^ flip) for z in range(4)]) for flip in range(1, 4)
    ]
    owns = pl.pallas_call(
        pack_trial_kernel,
        out_shape=[jax.ShapeDtypeStruct((rows, vecs // V_PARTS), trial.dtype)] * V_PARTS,
        in_specs=[SMEM, SMEM, VMEM],
        out_specs=[VMEM] * V_PARTS,
        compiler_params=room(4),
        name="pack_trial",
    )(at, block_live, trial)
    first_far = lax.ppermute(after(owns[0], *flags[1:]), "pair", FAR)
    live, pairs, which, large = pl.pallas_call(
        functools.partial(plan_kernel, classes),
        out_shape=[
            jax.ShapeDtypeStruct((4, blocks), jnp.int32),
            jax.ShapeDtypeStruct((4,), jnp.int32),
            jax.ShapeDtypeStruct((1,), jnp.int32),
            jax.ShapeDtypeStruct((1,), jnp.int32),
        ],
        in_specs=[SMEM] * 5,
        out_specs=[SMEM] * 4,
        compiler_params=room(2),
        name="plan",
    )(at, *flags)
    return lax.switch(
        which[0],
        [functools.partial(along_line, *pair, n_aux) for pair in classes],
        large,
        live,
        pairs,
        trial,
        energy_gap.reshape(blocks, BLK),
        factors,
        owns,
        first_far,
    )


def gathered(masked, factors, n_aux):
    everyone = lax.all_gather(masked, "pair", axis=0, tiled=True)
    rows = factors.reshape(-1, factors.shape[2])
    coeffs = exchange_sum(contract_rows(everyone, rows), n_aux)
    shares = lax.dot_general(
        rows, coeffs, (((1,), (1,)), ((), ())), preferred_element_type=jnp.float32
    )
    return lax.psum_scatter(
        shares.astype(jnp.bfloat16), "pair", scatter_dimension=0, tiled=True
    ).astype(jnp.float32)


def body(n_pair, n_aux, b_built, trial, energy_gap, block_live):
    blocks = trial.shape[0] // BLK
    aux = lax.axis_index("aux")
    if n_pair == 4:
        return on_four(n_aux, b_built[0], trial, energy_gap, block_live)
    own_blocks = lax.dynamic_slice_in_dim(block_live, aux * blocks, blocks, 0)
    own_live = jnp.repeat(own_blocks, BLK)
    masked = trial * own_live.astype(jnp.bfloat16)[:, None]
    response = gathered(masked, b_built[0], n_aux)
    base = energy_gap[:, None] * trial.astype(jnp.float32)
    return (base + 2.0 * own_live.astype(jnp.float32)[:, None] * response).astype(jnp.bfloat16)


def solution(mesh):
    sizes = [mesh.shape[axis] for axis in ("pair", "aux")]
    return jax.shard_map(
        functools.partial(body, *sizes),
        mesh=mesh,
        in_specs=(
            P(("traj", "aux"), None, None, "pair"),
            P(("traj", "pair", "aux"), "root"),
            P(("traj", "pair", "aux")),
            P(("traj", "pair")),
        ),
        out_specs=P(("traj", "pair", "aux"), "root"),
        check_vma=False,
    )
```

```python
import functools

import jax
import jax.numpy as jnp
from jax import lax
from jax.experimental import pallas as pl
from jax.experimental.pallas import tpu as pltpu
from jax.sharding import PartitionSpec as P

BLK = 128
V_PARTS = 2

SMEM = pl.BlockSpec(memory_space=pltpu.SMEM)
VMEM = pl.BlockSpec(memory_space=pltpu.VMEM)
ANY = pl.BlockSpec(memory_space=pl.ANY)


def contract_rows(left, right):
    return lax.dot_general(
        left, right, (((0,), (0,)), ((), ())), preferred_element_type=jnp.float32
    )


def exchange_sum(partial, n_aux):
    sent = partial.astype(jnp.bfloat16)
    if n_aux == 1:
        return sent
    if n_aux == 2:
        other = lax.ppermute(sent, "aux", [(0, 1), (1, 0)])
        return (partial + other.astype(jnp.float32)).astype(jnp.bfloat16)
    return lax.psum(sent, "aux")


def block_rows(block):
    return pl.ds(pl.multiple_of(block * BLK, BLK), BLK)


def plan_kernel(classes, at_ref, own_ref, near_ref, far_ref, opposite_ref, live_ref, pairs_ref, which_ref, large_ref):
    blocks = live_ref.shape[1]
    me = at_ref[0]

    def most(ref):
        top = jnp.int32(0)
        for group in range(ref.shape[0] // blocks):
            count = ref[group * blocks]
            for block in range(1, blocks):
                count = count + ref[group * blocks + block]
            top = jnp.maximum(top, count)
        return top

    alike = jnp.maximum(most(own_ref), most(opposite_ref))
    unlike = jnp.maximum(most(near_ref), most(far_ref))
    end = (me == 0) | (me == 3)
    ends_large = jnp.where(end, alike, unlike) >= jnp.where(end, unlike, alike)
    large = end == ends_large
    large_ref[0] = large.astype(jnp.int32)
    top, other = jnp.maximum(alike, unlike), jnp.minimum(alike, unlike)
    which = jnp.int32(len(classes) - 1)
    for at in range(len(classes) - 2, -1, -1):
        which = jnp.where((top <= classes[at][0]) & (other <= classes[at][1]), at, which)
    which_ref[0] = which
    rows = (((own_ref, 0), (far_ref, 2)), ((far_ref, 2), (own_ref, 0)), ((opposite_ref, 3), (near_ref, 1)), ((near_ref, 1), (opposite_ref, 3)))
    for row, ((if_large, large_flip), (if_small, small_flip)) in enumerate(rows):
        pairs_ref[row] = me ^ jnp.where(large, large_flip, small_flip)
        for block in range(blocks):
            at = at_ref[1] * blocks + block
            live_ref[row, block] = jnp.where(large, if_large[at], if_small[at])


def pack_trial_kernel(at_ref, live_ref, trial_ref, *out_refs):
    width = out_refs[0].shape[1]
    for out in out_refs:
        out[...] = jnp.zeros_like(out)
    slot = jnp.int32(0)
    blocks = trial_ref.shape[0] // BLK
    for block in range(blocks):
        here = live_ref[at_ref[1] * blocks + block]

        @pl.when(here > 0)
        def _(slot=slot, block=block):
            for part, out in enumerate(out_refs):
                out[block_rows(slot), :] = trial_ref[
                    pl.ds(block * BLK, BLK), pl.ds(part * width, width)
                ]

        slot = slot + here


def pack_factors_kernel(most, rest, live_ref, pairs_ref, factors_ref, own_ref, near_ref, index_ref, sems):
    blocks = live_ref.shape[1]
    copies = []
    places = ((own_ref, 0, most), (own_ref, most, rest), (near_ref, 0, most), (near_ref, most, rest))
    for row, (out, start, slots) in enumerate(places):
        for slot in range(blocks):
            index_ref[row, slot] = 0
        at = jnp.int32(0)
        for block in range(blocks):
            index_ref[row, at] = block
            at = at + live_ref[row, block]
        for slot in range(slots):
            copies.append(
                pltpu.make_async_copy(
                    factors_ref.at[pairs_ref[row], block_rows(index_ref[row, slot]), :],
                    out.at[pl.ds((start + slot) * BLK, BLK), :],
                    sems.at[row, slot],
                )
            )
            copies[-1].start()
    for copy in copies:
        copy.wait()


def base_kernel(gap_ref, trial_ref, *out_refs):
    width = out_refs[0].shape[1]
    for block in range(trial_ref.shape[0] // BLK):
        rows = pl.ds(block * BLK, BLK)
        gap = jnp.transpose(jnp.broadcast_to(gap_ref[pl.ds(block, 1), :], (width, BLK)))
        for part, out in enumerate(out_refs):
            out[rows, :] = gap * trial_ref[rows, pl.ds(part * width, width)].astype(jnp.float32)


def finish_kernel(most, large_ref, live_ref, base_ref, sum_ref, far_ref, *refs):
    out_ref = refs[-1]
    large = large_ref[0]
    start = (1 - large) * most
    slot = jnp.int32(0)
    for block in range(out_ref.shape[0] // BLK):
        rows = pl.ds(block * BLK, BLK)
        here = jnp.where(large > 0, live_ref[0, block], live_ref[1, block])

        @pl.when(here > 0)
        def _(slot=slot, rows=rows):
            response = sum_ref[block_rows(start + slot), :] + far_ref[block_rows(slot), :].astype(jnp.float32)
            out_ref[rows, :] = (base_ref[rows, :] + 2.0 * response).astype(out_ref.dtype)

        @pl.when(here == 0)
        def _(rows=rows):
            out_ref[rows, :] = base_ref[rows, :].astype(out_ref.dtype)

        slot = slot + here


NEAR = [(z, z ^ 1) for z in range(4)]
FAR = [(z, z ^ 2) for z in range(4)]


def room(mebibytes):
    return pltpu.CompilerParams(vmem_limit_bytes=mebibytes * 2**20)


def after(value, *others):
    return lax.optimization_barrier((value, *others))[0]


def along_line(most, rest, n_aux, large, live, pairs, trial, gap, factors, owns):
    rows, vecs = trial.shape
    width = vecs // V_PARTS
    is_large = large[0] > 0
    cut = most * BLK
    held = cut + rest * BLK
    owns = [own[:cut] for own in owns]

    def side(own, far):
        return jnp.concatenate(
            [jnp.where(is_large, own, far), jnp.where(is_large, far, own)[: held - cut]]
        )

    first_far = lax.ppermute(owns[0], "pair", FAR)
    own_factors, near_factors = pl.pallas_call(
        functools.partial(pack_factors_kernel, most, rest),
        out_shape=[jax.ShapeDtypeStruct((held, factors.shape[2]), factors.dtype)] * 2,
        in_specs=[SMEM, SMEM, ANY],
        out_specs=[VMEM, VMEM],
        scratch_shapes=[
            pltpu.SMEM((4, rows // BLK), jnp.int32),
            pltpu.SemaphoreType.DMA((4, most)),
        ],
        compiler_params=room(10),
        name="pack_factors",
    )(live, pairs, factors)
    bases = pl.pallas_call(
        base_kernel,
        out_shape=[jax.ShapeDtypeStruct((rows, width), jnp.float32)] * V_PARTS,
        in_specs=[VMEM, VMEM],
        out_specs=[VMEM] * V_PARTS,
        compiler_params=room(4),
        name="base",
    )(gap, trial)
    mine = [after(side(owns[0], first_far), own_factors, *bases)]
    theirs = [lax.ppermute(mine[0], "pair", NEAR)]
    second_far = lax.ppermute(after(owns[1], mine[0]), "pair", FAR)
    mine.append(side(owns[1], second_far))
    theirs.append(lax.ppermute(mine[1], "pair", NEAR))

    sigma = for_near = for_far = None
    for part in range(V_PARTS):
        got = theirs[part] if for_near is None else after(theirs[part], for_near)
        partial = contract_rows(mine[part], own_factors) + contract_rows(got, near_factors)
        coeffs = exchange_sum(partial, n_aux)
        if for_far is not None:
            coeffs = after(coeffs, for_far)

        def share(of):
            return lax.dot_general(
                of, coeffs, (((1,), (1,)), ((), ())), preferred_element_type=jnp.float32
            )

        for_near = share(near_factors).astype(jnp.bfloat16)
        got_near = lax.ppermute(for_near, "pair", NEAR)
        total = share(own_factors) + got_near.astype(jnp.float32)
        for_small = total[cut:]
        if most > rest:
            for_small = jnp.pad(for_small, ((0, 2 * cut - held), (0, 0)))
        for_far = jnp.where(is_large, for_small, total[:cut]).astype(jnp.bfloat16)
        got_far = lax.ppermute(for_far, "pair", FAR)
        first = sigma is None
        sigma = pl.pallas_call(
            functools.partial(finish_kernel, most),
            out_shape=jax.ShapeDtypeStruct((rows, vecs), trial.dtype),
            grid=(1,),
            in_specs=[SMEM, SMEM, VMEM, VMEM, VMEM] + ([] if first else [ANY]),
            out_specs=pl.BlockSpec((rows, width), lambda _, part=part: (0, part)),
            input_output_aliases={} if first else {5: 0},
            compiler_params=room(6),
            name="finish",
        )(large, live, bases[part], total, got_far, *([] if first else [sigma]))
    return sigma


def on_four(n_aux, factors, trial, energy_gap, block_live):
    rows, vecs = trial.shape
    blocks = rows // BLK
    classes = [pair for pair in ((6, 3), (6, 4), (7, 4)) if max(pair) < blocks] + [(blocks, blocks)]
    at = jnp.stack([lax.axis_index("pair"), lax.axis_index("aux")]).astype(jnp.int32)
    flags = [block_live] + [
        lax.ppermute(block_live, "pair", [(z, z ^ flip) for z in range(4)]) for flip in range(1, 4)
    ]
    owns = pl.pallas_call(
        pack_trial_kernel,
        out_shape=[jax.ShapeDtypeStruct((rows, vecs // V_PARTS), trial.dtype)] * V_PARTS,
        in_specs=[SMEM, SMEM, VMEM],
        out_specs=[VMEM] * V_PARTS,
        compiler_params=room(4),
        name="pack_trial",
    )(at, block_live, trial)
    live, pairs, which, large = pl.pallas_call(
        functools.partial(plan_kernel, classes),
        out_shape=[
            jax.ShapeDtypeStruct((4, blocks), jnp.int32),
            jax.ShapeDtypeStruct((4,), jnp.int32),
            jax.ShapeDtypeStruct((1,), jnp.int32),
            jax.ShapeDtypeStruct((1,), jnp.int32),
        ],
        in_specs=[SMEM] * 5,
        out_specs=[SMEM] * 4,
        compiler_params=room(2),
        name="plan",
    )(at, *flags)
    return lax.switch(
        which[0],
        [functools.partial(along_line, *pair, n_aux) for pair in classes],
        large,
        live,
        pairs,
        trial,
        energy_gap.reshape(blocks, BLK),
        factors,
        owns,
    )


def gathered(masked, factors, n_aux):
    everyone = lax.all_gather(masked, "pair", axis=0, tiled=True)
    rows = factors.reshape(-1, factors.shape[2])
    coeffs = exchange_sum(contract_rows(everyone, rows), n_aux)
    shares = lax.dot_general(
        rows, coeffs, (((1,), (1,)), ((), ())), preferred_element_type=jnp.float32
    )
    return lax.psum_scatter(
        shares.astype(jnp.bfloat16), "pair", scatter_dimension=0, tiled=True
    ).astype(jnp.float32)


def body(n_pair, n_aux, b_built, trial, energy_gap, block_live):
    blocks = trial.shape[0] // BLK
    aux = lax.axis_index("aux")
    if n_pair == 4:
        return on_four(n_aux, b_built[0], trial, energy_gap, block_live)
    own_blocks = lax.dynamic_slice_in_dim(block_live, aux * blocks, blocks, 0)
    own_live = jnp.repeat(own_blocks, BLK)
    masked = trial * own_live.astype(jnp.bfloat16)[:, None]
    response = gathered(masked, b_built[0], n_aux)
    base = energy_gap[:, None] * trial.astype(jnp.float32)
    return (base + 2.0 * own_live.astype(jnp.float32)[:, None] * response).astype(jnp.bfloat16)


def solution(mesh):
    sizes = [mesh.shape[axis] for axis in ("pair", "aux")]
    return jax.shard_map(
        functools.partial(body, *sizes),
        mesh=mesh,
        in_specs=(
            P(("traj", "aux"), None, None, "pair"),
            P(("traj", "pair", "aux"), "root"),
            P(("traj", "pair", "aux")),
            P(("traj", "pair")),
        ),
        out_specs=P(("traj", "pair", "aux"), "root"),
        check_vma=False,
    )
```

```python
import functools

import jax
import jax.numpy as jnp
from jax import lax
from jax.experimental import pallas as pl
from jax.experimental.pallas import tpu as pltpu
from jax.sharding import PartitionSpec as P

BLK = 128
V_PARTS = 2

SMEM = pl.BlockSpec(memory_space=pltpu.SMEM)
VMEM = pl.BlockSpec(memory_space=pltpu.VMEM)
ANY = pl.BlockSpec(memory_space=pl.ANY)


def contract_rows(left, right):
    return lax.dot_general(
        left, right, (((0,), (0,)), ((), ())), preferred_element_type=jnp.float32
    )


def exchange_sum(partial, n_aux):
    sent = partial.astype(jnp.bfloat16)
    if n_aux == 1:
        return sent
    if n_aux == 2:
        other = lax.ppermute(sent, "aux", [(0, 1), (1, 0)])
        return (partial + other.astype(jnp.float32)).astype(jnp.bfloat16)
    return lax.psum(sent, "aux")


def block_rows(block):
    return pl.ds(pl.multiple_of(block * BLK, BLK), BLK)


def plan_kernel(classes, at_ref, own_ref, near_ref, far_ref, opposite_ref, live_ref, pairs_ref, which_ref, large_ref):
    blocks = live_ref.shape[1]
    me = at_ref[0]

    def most(ref):
        top = jnp.int32(0)
        for group in range(ref.shape[0] // blocks):
            count = ref[group * blocks]
            for block in range(1, blocks):
                count = count + ref[group * blocks + block]
            top = jnp.maximum(top, count)
        return top

    alike = jnp.maximum(most(own_ref), most(opposite_ref))
    unlike = jnp.maximum(most(near_ref), most(far_ref))
    end = (me == 0) | (me == 3)
    ends_large = jnp.where(end, alike, unlike) >= jnp.where(end, unlike, alike)
    large = end == ends_large
    large_ref[0] = large.astype(jnp.int32)
    top, other = jnp.maximum(alike, unlike), jnp.minimum(alike, unlike)
    which = jnp.int32(len(classes) - 1)
    for at in range(len(classes) - 2, -1, -1):
        which = jnp.where((top <= classes[at][0]) & (other <= classes[at][1]), at, which)
    which_ref[0] = which
    rows = (((own_ref, 0), (far_ref, 2)), ((far_ref, 2), (own_ref, 0)), ((opposite_ref, 3), (near_ref, 1)), ((near_ref, 1), (opposite_ref, 3)))
    for row, ((if_large, large_flip), (if_small, small_flip)) in enumerate(rows):
        pairs_ref[row] = me ^ jnp.where(large, large_flip, small_flip)
        for block in range(blocks):
            at = at_ref[1] * blocks + block
            live_ref[row, block] = jnp.where(large, if_large[at], if_small[at])


def pack_trial_kernel(at_ref, live_ref, trial_ref, *out_refs):
    width = out_refs[0].shape[1]
    for out in out_refs:
        out[...] = jnp.zeros_like(out)
    slot = jnp.int32(0)
    blocks = trial_ref.shape[0] // BLK
    for block in range(blocks):
        here = live_ref[at_ref[1] * blocks + block]

        @pl.when(here > 0)
        def _(slot=slot, block=block):
            for part, out in enumerate(out_refs):
                out[block_rows(slot), :] = trial_ref[
                    pl.ds(block * BLK, BLK), pl.ds(part * width, width)
                ]

        slot = slot + here


def pack_factors_kernel(most, rest, large_ref, live_ref, pairs_ref, factors_ref, *refs):
    outs, (index_ref, sems) = refs[:4], refs[4:]
    blocks = live_ref.shape[1]
    for row in range(4):
        for slot in range(blocks):
            index_ref[row, slot] = 0
        at = jnp.int32(0)
        for block in range(blocks):
            index_ref[row, at] = block
            at = at + live_ref[row, block]
    large = large_ref[0]
    turned = 2 * (1 - large)
    rows = ((0, 1), (2, 3), (turned, 3 - turned), (2 - turned, 1 + turned))
    copies = []
    for at, (out, pieces) in enumerate(zip(outs, rows)):
        for piece, (row, start, slots) in enumerate(zip(pieces, (0, most), (most, rest))):
            for slot in range(slots):
                copies.append(
                    pltpu.make_async_copy(
                        factors_ref.at[pairs_ref[row], block_rows(index_ref[row, slot]), :],
                        out.at[pl.ds((start + slot) * BLK, BLK), :],
                        sems.at[2 * at + piece, slot],
                    )
                )
                copies[-1].start()
    for copy in copies:
        copy.wait()


def base_kernel(gap_ref, trial_ref, *out_refs):
    width = out_refs[0].shape[1]
    for block in range(trial_ref.shape[0] // BLK):
        rows = pl.ds(block * BLK, BLK)
        gap = jnp.transpose(jnp.broadcast_to(gap_ref[pl.ds(block, 1), :], (width, BLK)))
        for part, out in enumerate(out_refs):
            out[rows, :] = gap * trial_ref[rows, pl.ds(part * width, width)].astype(jnp.float32)


def finish_kernel(most, large_ref, live_ref, base_ref, sum_ref, far_ref, *refs):
    out_ref = refs[-1]
    large = large_ref[0]
    start = (1 - large) * most
    slot = jnp.int32(0)
    for block in range(out_ref.shape[0] // BLK):
        rows = pl.ds(block * BLK, BLK)
        here = jnp.where(large > 0, live_ref[0, block], live_ref[1, block])

        @pl.when(here > 0)
        def _(slot=slot, rows=rows):
            response = sum_ref[block_rows(start + slot), :] + far_ref[block_rows(slot), :].astype(jnp.float32)
            out_ref[rows, :] = (base_ref[rows, :] + 2.0 * response).astype(out_ref.dtype)

        @pl.when(here == 0)
        def _(rows=rows):
            out_ref[rows, :] = base_ref[rows, :].astype(out_ref.dtype)

        slot = slot + here


NEAR = [(z, z ^ 1) for z in range(4)]
FAR = [(z, z ^ 2) for z in range(4)]


def room(mebibytes):
    return pltpu.CompilerParams(vmem_limit_bytes=mebibytes * 2**20)


def after(value, *others):
    return lax.optimization_barrier((value, *others))[0]


def along_line(most, rest, n_aux, large, live, pairs, trial, gap, factors, owns):
    rows, vecs = trial.shape
    width = vecs // V_PARTS
    is_large = large[0] > 0
    cut = most * BLK
    held = cut + rest * BLK
    owns = [own[:cut] for own in owns]
    steps = ((FAR, NEAR), (NEAR, FAR))

    def side(own, got):
        return jnp.concatenate(
            [jnp.where(is_large, own, got), jnp.where(is_large, got, own)[: held - cut]]
        )

    firsts = [lax.ppermute(own, "pair", step[0]) for own, step in zip(owns, steps)]
    packed = pl.pallas_call(
        functools.partial(pack_factors_kernel, most, rest),
        out_shape=[jax.ShapeDtypeStruct((held, factors.shape[2]), factors.dtype)] * 4,
        in_specs=[SMEM, SMEM, SMEM, ANY],
        out_specs=[VMEM] * 4,
        scratch_shapes=[
            pltpu.SMEM((4, rows // BLK), jnp.int32),
            pltpu.SemaphoreType.DMA((8, most)),
        ],
        compiler_params=room(12),
        name="pack_factors",
    )(large, live, pairs, factors)
    bases = pl.pallas_call(
        base_kernel,
        out_shape=[jax.ShapeDtypeStruct((rows, width), jnp.float32)] * V_PARTS,
        in_specs=[VMEM, VMEM],
        out_specs=[VMEM] * V_PARTS,
        compiler_params=room(4),
        name="base",
    )(gap, trial)
    mine = [after(side(own, got), *packed, *bases) for own, got in zip(owns, firsts)]
    theirs = [lax.ppermute(held_here, "pair", step[1]) for held_here, step in zip(mine, steps)]

    sigma = partial = None
    for part, (first_step, second_step) in enumerate(steps):
        own_factors, other_factors = packed[2 * part : 2 * part + 2]
        got = theirs[part] if partial is None else after(theirs[part], partial)
        partial = contract_rows(mine[part], own_factors) + contract_rows(got, other_factors)
        coeffs = exchange_sum(partial, n_aux)

        def share(of):
            return lax.dot_general(
                of, coeffs, (((1,), (1,)), ((), ())), preferred_element_type=jnp.float32
            )

        got = lax.ppermute(share(other_factors).astype(jnp.bfloat16), "pair", second_step)
        total = share(own_factors) + got.astype(jnp.float32)
        for_small = total[cut:]
        if most > rest:
            for_small = jnp.pad(for_small, ((0, 2 * cut - held), (0, 0)))
        away = jnp.where(is_large, for_small, total[:cut]).astype(jnp.bfloat16)
        got = lax.ppermute(away, "pair", first_step)
        begun = sigma is not None
        sigma = pl.pallas_call(
            functools.partial(finish_kernel, most),
            out_shape=jax.ShapeDtypeStruct((rows, vecs), trial.dtype),
            grid=(1,),
            in_specs=[SMEM, SMEM, VMEM, VMEM, VMEM] + ([ANY] if begun else []),
            out_specs=pl.BlockSpec((rows, width), lambda _, part=part: (0, part)),
            input_output_aliases={5: 0} if begun else {},
            compiler_params=room(6),
            name="finish",
        )(large, live, bases[part], total, got, *([sigma] if begun else []))
    return sigma


def on_four(n_aux, factors, trial, energy_gap, block_live):
    rows, vecs = trial.shape
    blocks = rows // BLK
    classes = [pair for pair in ((6, 3), (6, 4), (7, 4)) if max(pair) < blocks] + [(blocks, blocks)]
    at = jnp.stack([lax.axis_index("pair"), lax.axis_index("aux")]).astype(jnp.int32)
    owns = pl.pallas_call(
        pack_trial_kernel,
        out_shape=[jax.ShapeDtypeStruct((rows, vecs // V_PARTS), trial.dtype)] * V_PARTS,
        in_specs=[SMEM, SMEM, VMEM],
        out_specs=[VMEM] * V_PARTS,
        compiler_params=room(4),
        name="pack_trial",
    )(at, block_live, trial)
    sent = after(block_live, *owns)
    flags = [block_live] + [
        lax.ppermute(sent, "pair", [(z, z ^ flip) for z in range(4)]) for flip in range(1, 4)
    ]
    live, pairs, which, large = pl.pallas_call(
        functools.partial(plan_kernel, classes),
        out_shape=[
            jax.ShapeDtypeStruct((4, blocks), jnp.int32),
            jax.ShapeDtypeStruct((4,), jnp.int32),
            jax.ShapeDtypeStruct((1,), jnp.int32),
            jax.ShapeDtypeStruct((1,), jnp.int32),
        ],
        in_specs=[SMEM] * 5,
        out_specs=[SMEM] * 4,
        compiler_params=room(2),
        name="plan",
    )(at, *flags)
    return lax.switch(
        which[0],
        [functools.partial(along_line, *pair, n_aux) for pair in classes],
        large,
        live,
        pairs,
        trial,
        energy_gap.reshape(blocks, BLK),
        factors,
        owns,
    )


def gathered(masked, factors, n_aux):
    everyone = lax.all_gather(masked, "pair", axis=0, tiled=True)
    rows = factors.reshape(-1, factors.shape[2])
    coeffs = exchange_sum(contract_rows(everyone, rows), n_aux)
    shares = lax.dot_general(
        rows, coeffs, (((1,), (1,)), ((), ())), preferred_element_type=jnp.float32
    )
    return lax.psum_scatter(
        shares.astype(jnp.bfloat16), "pair", scatter_dimension=0, tiled=True
    ).astype(jnp.float32)


def body(n_pair, n_aux, b_built, trial, energy_gap, block_live):
    blocks = trial.shape[0] // BLK
    aux = lax.axis_index("aux")
    if n_pair == 4:
        return on_four(n_aux, b_built[0], trial, energy_gap, block_live)
    own_blocks = lax.dynamic_slice_in_dim(block_live, aux * blocks, blocks, 0)
    own_live = jnp.repeat(own_blocks, BLK)
    masked = trial * own_live.astype(jnp.bfloat16)[:, None]
    response = gathered(masked, b_built[0], n_aux)
    base = energy_gap[:, None] * trial.astype(jnp.float32)
    return (base + 2.0 * own_live.astype(jnp.float32)[:, None] * response).astype(jnp.bfloat16)


def solution(mesh):
    sizes = [mesh.shape[axis] for axis in ("pair", "aux")]
    return jax.shard_map(
        functools.partial(body, *sizes),
        mesh=mesh,
        in_specs=(
            P(("traj", "aux"), None, None, "pair"),
            P(("traj", "pair", "aux"), "root"),
            P(("traj", "pair", "aux")),
            P(("traj", "pair")),
        ),
        out_specs=P(("traj", "pair", "aux"), "root"),
        check_vma=False,
    )
```

```python
import functools

import jax
import jax.numpy as jnp
from jax import lax
from jax.experimental import pallas as pl
from jax.experimental.pallas import tpu as pltpu
from jax.sharding import PartitionSpec as P

BLK = 128
V_PARTS = 2

SMEM = pl.BlockSpec(memory_space=pltpu.SMEM)
VMEM = pl.BlockSpec(memory_space=pltpu.VMEM)
ANY = pl.BlockSpec(memory_space=pl.ANY)


def contract_rows(left, right):
    return lax.dot_general(
        left, right, (((0,), (0,)), ((), ())), preferred_element_type=jnp.float32
    )


def exchange_sum(partial, n_aux):
    sent = partial.astype(jnp.bfloat16)
    if n_aux == 1:
        return sent
    if n_aux == 2:
        other = lax.ppermute(sent, "aux", [(0, 1), (1, 0)])
        return (partial + other.astype(jnp.float32)).astype(jnp.bfloat16)
    return lax.psum(sent, "aux")


def block_rows(block):
    return pl.ds(pl.multiple_of(block * BLK, BLK), BLK)


def plan_kernel(classes, at_ref, own_ref, near_ref, far_ref, opposite_ref, live_ref, pairs_ref, which_ref, large_ref):
    blocks = live_ref.shape[1]
    me = at_ref[0]

    def most(ref):
        top = jnp.int32(0)
        for group in range(ref.shape[0] // blocks):
            count = ref[group * blocks]
            for block in range(1, blocks):
                count = count + ref[group * blocks + block]
            top = jnp.maximum(top, count)
        return top

    alike = jnp.maximum(most(own_ref), most(opposite_ref))
    unlike = jnp.maximum(most(near_ref), most(far_ref))
    end = (me == 0) | (me == 3)
    ends_large = jnp.where(end, alike, unlike) >= jnp.where(end, unlike, alike)
    large = end == ends_large
    large_ref[0] = large.astype(jnp.int32)
    top, other = jnp.maximum(alike, unlike), jnp.minimum(alike, unlike)
    which = jnp.int32(len(classes) - 1)
    for at in range(len(classes) - 2, -1, -1):
        which = jnp.where((top <= classes[at][0]) & (other <= classes[at][1]), at, which)
    which_ref[0] = which
    rows = (((own_ref, 0), (far_ref, 2)), ((far_ref, 2), (own_ref, 0)), ((opposite_ref, 3), (near_ref, 1)), ((near_ref, 1), (opposite_ref, 3)))
    for row, ((if_large, large_flip), (if_small, small_flip)) in enumerate(rows):
        pairs_ref[row] = me ^ jnp.where(large, large_flip, small_flip)
        for block in range(blocks):
            at = at_ref[1] * blocks + block
            live_ref[row, block] = jnp.where(large, if_large[at], if_small[at])


def pack_trial_kernel(at_ref, live_ref, trial_ref, *out_refs):
    width = out_refs[0].shape[1]
    for out in out_refs:
        out[...] = jnp.zeros_like(out)
    slot = jnp.int32(0)
    blocks = trial_ref.shape[0] // BLK
    for block in range(blocks):
        here = live_ref[at_ref[1] * blocks + block]

        @pl.when(here > 0)
        def _(slot=slot, block=block):
            for part, out in enumerate(out_refs):
                out[block_rows(slot), :] = trial_ref[
                    pl.ds(block * BLK, BLK), pl.ds(part * width, width)
                ]

        slot = slot + here


def pack_factors_kernel(most, rest, half, large_ref, live_ref, pairs_ref, factors_ref, own_ref, other_ref, index_ref, sems):
    blocks = live_ref.shape[1]
    for row in range(4):
        for slot in range(blocks):
            index_ref[row, slot] = 0
        at = jnp.int32(0)
        for block in range(blocks):
            index_ref[row, at] = block
            at = at + live_ref[row, block]
    turned = 2 * (1 - large_ref[0])
    rows = (((0, 1), (2, 3)), ((turned, 3 - turned), (2 - turned, 1 + turned)))[half]
    copies = []
    for at, (out, pieces) in enumerate(zip((own_ref, other_ref), rows)):
        for piece, (row, start, slots) in enumerate(zip(pieces, (0, most), (most, rest))):
            for slot in range(slots):
                copies.append(
                    pltpu.make_async_copy(
                        factors_ref.at[pairs_ref[row], block_rows(index_ref[row, slot]), :],
                        out.at[pl.ds((start + slot) * BLK, BLK), :],
                        sems.at[2 * at + piece, slot],
                    )
                )
                copies[-1].start()
    for copy in copies:
        copy.wait()


def base_kernel(gap_ref, trial_ref, *out_refs):
    width = out_refs[0].shape[1]
    for block in range(trial_ref.shape[0] // BLK):
        rows = pl.ds(block * BLK, BLK)
        gap = jnp.transpose(jnp.broadcast_to(gap_ref[pl.ds(block, 1), :], (width, BLK)))
        for part, out in enumerate(out_refs):
            out[rows, :] = gap * trial_ref[rows, pl.ds(part * width, width)].astype(jnp.float32)


def finish_kernel(most, large_ref, live_ref, base_ref, sum_ref, far_ref, *refs):
    out_ref = refs[-1]
    large = large_ref[0]
    start = (1 - large) * most
    slot = jnp.int32(0)
    for block in range(out_ref.shape[0] // BLK):
        rows = pl.ds(block * BLK, BLK)
        here = jnp.where(large > 0, live_ref[0, block], live_ref[1, block])

        @pl.when(here > 0)
        def _(slot=slot, rows=rows):
            response = sum_ref[block_rows(start + slot), :] + far_ref[block_rows(slot), :].astype(jnp.float32)
            out_ref[rows, :] = (base_ref[rows, :] + 2.0 * response).astype(out_ref.dtype)

        @pl.when(here == 0)
        def _(rows=rows):
            out_ref[rows, :] = base_ref[rows, :].astype(out_ref.dtype)

        slot = slot + here


NEAR = [(z, z ^ 1) for z in range(4)]
FAR = [(z, z ^ 2) for z in range(4)]


def room(mebibytes):
    return pltpu.CompilerParams(vmem_limit_bytes=mebibytes * 2**20)


def after(value, *others):
    return lax.optimization_barrier((value, *others))[0]


def along_line(most, rest, n_aux, large, live, pairs, trial, gap, factors, owns):
    rows, vecs = trial.shape
    width = vecs // V_PARTS
    is_large = large[0] > 0
    cut = most * BLK
    held = cut + rest * BLK
    owns = [own[:cut] for own in owns]
    steps = ((FAR, NEAR), (NEAR, FAR))

    def side(own, got):
        return jnp.concatenate(
            [jnp.where(is_large, own, got), jnp.where(is_large, got, own)[: held - cut]]
        )

    firsts = [lax.ppermute(own, "pair", step[0]) for own, step in zip(owns, steps)]
    packed = [
        pl.pallas_call(
            functools.partial(pack_factors_kernel, most, rest, part),
            out_shape=[jax.ShapeDtypeStruct((held, factors.shape[2]), factors.dtype)] * 2,
            in_specs=[SMEM, SMEM, SMEM, ANY],
            out_specs=[VMEM] * 2,
            scratch_shapes=[
                pltpu.SMEM((4, rows // BLK), jnp.int32),
                pltpu.SemaphoreType.DMA((4, most)),
            ],
            compiler_params=room(8),
            name="pack_factors",
        )(large, live, pairs, factors)
        for part in range(V_PARTS)
    ]
    bases = pl.pallas_call(
        base_kernel,
        out_shape=[jax.ShapeDtypeStruct((rows, width), jnp.float32)] * V_PARTS,
        in_specs=[VMEM, VMEM],
        out_specs=[VMEM] * V_PARTS,
        compiler_params=room(4),
        name="base",
    )(gap, trial)
    mine = [after(side(own, got), *packed[0]) for own, got in zip(owns, firsts)]
    theirs = [lax.ppermute(held_here, "pair", step[1]) for held_here, step in zip(mine, steps)]
    theirs[0] = after(theirs[0], *packed[1], *bases)

    totals, aways = [], []
    partial = None
    for part, (first_step, second_step) in enumerate(steps):
        own_factors, other_factors = packed[part]
        got = theirs[part] if partial is None else after(theirs[part], partial)
        partial = contract_rows(mine[part], own_factors) + contract_rows(got, other_factors)
        coeffs = exchange_sum(partial, n_aux)

        def share(of):
            return lax.dot_general(
                of, coeffs, (((1,), (1,)), ((), ())), preferred_element_type=jnp.float32
            )

        got = lax.ppermute(share(other_factors).astype(jnp.bfloat16), "pair", second_step)
        total = share(own_factors) + got.astype(jnp.float32)
        for_small = total[cut:]
        if most > rest:
            for_small = jnp.pad(for_small, ((0, 2 * cut - held), (0, 0)))
        totals.append(total)
        aways.append(jnp.where(is_large, for_small, total[:cut]).astype(jnp.bfloat16))
    aways[0] = after(aways[0], aways[1])
    sigma = None
    for part in reversed(range(V_PARTS)):
        got = lax.ppermute(aways[part], "pair", steps[part][0])
        begun = sigma is not None
        sigma = pl.pallas_call(
            functools.partial(finish_kernel, most),
            out_shape=jax.ShapeDtypeStruct((rows, vecs), trial.dtype),
            grid=(1,),
            in_specs=[SMEM, SMEM, VMEM, VMEM, VMEM] + ([ANY] if begun else []),
            out_specs=pl.BlockSpec((rows, width), lambda _, part=part: (0, part)),
            input_output_aliases={5: 0} if begun else {},
            compiler_params=room(6),
            name="finish",
        )(large, live, bases[part], totals[part], got, *([sigma] if begun else []))
    return sigma


def on_four(n_aux, factors, trial, energy_gap, block_live):
    rows, vecs = trial.shape
    blocks = rows // BLK
    classes = [pair for pair in ((6, 3), (6, 4), (7, 4)) if max(pair) < blocks] + [(blocks, blocks)]
    at = jnp.stack([lax.axis_index("pair"), lax.axis_index("aux")]).astype(jnp.int32)
    flags = [block_live] + [
        lax.ppermute(block_live, "pair", [(z, z ^ flip) for z in range(4)]) for flip in range(1, 4)
    ]
    owns = pl.pallas_call(
        pack_trial_kernel,
        out_shape=[jax.ShapeDtypeStruct((rows, vecs // V_PARTS), trial.dtype)] * V_PARTS,
        in_specs=[SMEM, SMEM, VMEM],
        out_specs=[VMEM] * V_PARTS,
        name="pack_trial",
    )(at, block_live, trial)
    live, pairs, which, large = pl.pallas_call(
        functools.partial(plan_kernel, classes),
        out_shape=[
            jax.ShapeDtypeStruct((4, blocks), jnp.int32),
            jax.ShapeDtypeStruct((4,), jnp.int32),
            jax.ShapeDtypeStruct((1,), jnp.int32),
            jax.ShapeDtypeStruct((1,), jnp.int32),
        ],
        in_specs=[SMEM] * 5,
        out_specs=[SMEM] * 4,
        compiler_params=room(2),
        name="plan",
    )(at, *flags)
    return lax.switch(
        which[0],
        [functools.partial(along_line, *pair, n_aux) for pair in classes],
        large,
        live,
        pairs,
        trial,
        energy_gap.reshape(blocks, BLK),
        factors,
        owns,
    )


def gathered(masked, factors, n_aux):
    everyone = lax.all_gather(masked, "pair", axis=0, tiled=True)
    rows = factors.reshape(-1, factors.shape[2])
    coeffs = exchange_sum(contract_rows(everyone, rows), n_aux)
    shares = lax.dot_general(
        rows, coeffs, (((1,), (1,)), ((), ())), preferred_element_type=jnp.float32
    )
    return lax.psum_scatter(
        shares.astype(jnp.bfloat16), "pair", scatter_dimension=0, tiled=True
    ).astype(jnp.float32)


def body(n_pair, n_aux, b_built, trial, energy_gap, block_live):
    blocks = trial.shape[0] // BLK
    aux = lax.axis_index("aux")
    if n_pair == 4:
        return on_four(n_aux, b_built[0], trial, energy_gap, block_live)
    own_blocks = lax.dynamic_slice_in_dim(block_live, aux * blocks, blocks, 0)
    own_live = jnp.repeat(own_blocks, BLK)
    masked = trial * own_live.astype(jnp.bfloat16)[:, None]
    response = gathered(masked, b_built[0], n_aux)
    base = energy_gap[:, None] * trial.astype(jnp.float32)
    return (base + 2.0 * own_live.astype(jnp.float32)[:, None] * response).astype(jnp.bfloat16)


def solution(mesh):
    sizes = [mesh.shape[axis] for axis in ("pair", "aux")]
    return jax.shard_map(
        functools.partial(body, *sizes),
        mesh=mesh,
        in_specs=(
            P(("traj", "aux"), None, None, "pair"),
            P(("traj", "pair", "aux"), "root"),
            P(("traj", "pair", "aux")),
            P(("traj", "pair")),
        ),
        out_specs=P(("traj", "pair", "aux"), "root"),
        check_vma=False,
    )
```

```python
import functools

import jax
import jax.numpy as jnp
from jax import lax
from jax.experimental import pallas as pl
from jax.experimental.pallas import tpu as pltpu
from jax.sharding import PartitionSpec as P

BLK = 128
V_PARTS = 2

SMEM = pl.BlockSpec(memory_space=pltpu.SMEM)
VMEM = pl.BlockSpec(memory_space=pltpu.VMEM)
ANY = pl.BlockSpec(memory_space=pl.ANY)


def contract_rows(left, right):
    return lax.dot_general(
        left, right, (((0,), (0,)), ((), ())), preferred_element_type=jnp.float32
    )


def exchange_sum(partial, n_aux):
    sent = partial.astype(jnp.bfloat16)
    if n_aux == 1:
        return sent
    if n_aux == 2:
        other = lax.ppermute(sent, "aux", [(0, 1), (1, 0)])
        return (partial + other.astype(jnp.float32)).astype(jnp.bfloat16)
    return lax.psum(sent, "aux")


def block_rows(block):
    return pl.ds(pl.multiple_of(block * BLK, BLK), BLK)


def pack_trial(at_ref, live_ref, trial_ref, out_refs):
    width = out_refs[0].shape[1]
    for out in out_refs:
        out[...] = jnp.zeros_like(out)
    slot = jnp.int32(0)
    blocks = trial_ref.shape[0] // BLK
    for block in range(blocks):
        here = live_ref[at_ref[1] * blocks + block]

        @pl.when(here > 0)
        def _(slot=slot, block=block):
            for part, out in enumerate(out_refs):
                out[block_rows(slot), :] = trial_ref[
                    pl.ds(block * BLK, BLK), pl.ds(part * width, width)
                ]

        slot = slot + here


def plan_kernel(classes, at_ref, own_ref, near_ref, far_ref, opposite_ref, trial_ref, live_ref, pairs_ref, which_ref, large_ref, *out_refs):
    pack_trial(at_ref, own_ref, trial_ref, out_refs)
    blocks = live_ref.shape[1]
    me = at_ref[0]

    def most(ref):
        top = jnp.int32(0)
        for group in range(ref.shape[0] // blocks):
            count = ref[group * blocks]
            for block in range(1, blocks):
                count = count + ref[group * blocks + block]
            top = jnp.maximum(top, count)
        return top

    alike = jnp.maximum(most(own_ref), most(opposite_ref))
    unlike = jnp.maximum(most(near_ref), most(far_ref))
    end = (me == 0) | (me == 3)
    ends_large = jnp.where(end, alike, unlike) >= jnp.where(end, unlike, alike)
    large = end == ends_large
    large_ref[0] = large.astype(jnp.int32)
    top, other = jnp.maximum(alike, unlike), jnp.minimum(alike, unlike)
    which = jnp.int32(len(classes) - 1)
    for at in range(len(classes) - 2, -1, -1):
        which = jnp.where((top <= classes[at][0]) & (other <= classes[at][1]), at, which)
    which_ref[0] = which
    rows = (((own_ref, 0), (far_ref, 2)), ((far_ref, 2), (own_ref, 0)), ((opposite_ref, 3), (near_ref, 1)), ((near_ref, 1), (opposite_ref, 3)))
    for row, ((if_large, large_flip), (if_small, small_flip)) in enumerate(rows):
        pairs_ref[row] = me ^ jnp.where(large, large_flip, small_flip)
        for block in range(blocks):
            at = at_ref[1] * blocks + block
            live_ref[row, block] = jnp.where(large, if_large[at], if_small[at])


def pack_factors_kernel(most, rest, large_ref, live_ref, pairs_ref, factors_ref, *refs):
    outs, (index_ref, sems) = refs[:4], refs[4:]
    blocks = live_ref.shape[1]
    for row in range(4):
        for slot in range(blocks):
            index_ref[row, slot] = 0
        at = jnp.int32(0)
        for block in range(blocks):
            index_ref[row, at] = block
            at = at + live_ref[row, block]
    large = large_ref[0]
    turned = 2 * (1 - large)
    rows = ((0, 1), (2, 3), (turned, 3 - turned), (2 - turned, 1 + turned))
    copies = []
    for at, (out, pieces) in enumerate(zip(outs, rows)):
        for piece, (row, start, slots) in enumerate(zip(pieces, (0, most), (most, rest))):
            for slot in range(slots):
                copies.append(
                    pltpu.make_async_copy(
                        factors_ref.at[pairs_ref[row], block_rows(index_ref[row, slot]), :],
                        out.at[pl.ds((start + slot) * BLK, BLK), :],
                        sems.at[2 * at + piece, slot],
                    )
                )
                copies[-1].start()
    for copy in copies:
        copy.wait()


def base_kernel(gap_ref, trial_ref, *out_refs):
    width = out_refs[0].shape[1]
    for block in range(trial_ref.shape[0] // BLK):
        rows = pl.ds(block * BLK, BLK)
        gap = jnp.transpose(jnp.broadcast_to(gap_ref[pl.ds(block, 1), :], (width, BLK)))
        for part, out in enumerate(out_refs):
            out[rows, :] = gap * trial_ref[rows, pl.ds(part * width, width)].astype(jnp.float32)


def finish_kernel(most, large_ref, live_ref, *refs):
    parts = len(refs) // 3
    bases, totals, lasts, out_ref = refs[:parts], refs[parts : 2 * parts], refs[2 * parts : 3 * parts], refs[-1]
    width = out_ref.shape[1] // parts
    large = large_ref[0]
    start = (1 - large) * most
    slot = jnp.int32(0)
    for block in range(out_ref.shape[0] // BLK):
        rows = pl.ds(block * BLK, BLK)
        here = jnp.where(large > 0, live_ref[0, block], live_ref[1, block])

        @pl.when(here > 0)
        def _(slot=slot, rows=rows):
            for part in range(parts):
                last = lasts[part][block_rows(slot), :].astype(jnp.float32)
                response = totals[part][block_rows(start + slot), :] + last
                out_ref[rows, pl.ds(part * width, width)] = (
                    bases[part][rows, :] + 2.0 * response
                ).astype(out_ref.dtype)

        @pl.when(here == 0)
        def _(rows=rows):
            for part in range(parts):
                out_ref[rows, pl.ds(part * width, width)] = bases[part][rows, :].astype(out_ref.dtype)

        slot = slot + here


NEAR = [(z, z ^ 1) for z in range(4)]
FAR = [(z, z ^ 2) for z in range(4)]


def room(mebibytes):
    return pltpu.CompilerParams(vmem_limit_bytes=mebibytes * 2**20)


def after(value, *others):
    return lax.optimization_barrier((value, *others))[0]


def along_line(most, rest, n_aux, large, live, pairs, trial, gap, factors, owns):
    rows, vecs = trial.shape
    width = vecs // V_PARTS
    is_large = large[0] > 0
    cut = most * BLK
    held = cut + rest * BLK
    owns = [own[:cut] for own in owns]
    steps = ((FAR, NEAR), (NEAR, FAR))

    def side(own, got):
        return jnp.concatenate(
            [jnp.where(is_large, own, got), jnp.where(is_large, got, own)[: held - cut]]
        )

    firsts = [lax.ppermute(own, "pair", step[0]) for own, step in zip(owns, steps)]
    packed = pl.pallas_call(
        functools.partial(pack_factors_kernel, most, rest),
        out_shape=[jax.ShapeDtypeStruct((held, factors.shape[2]), factors.dtype)] * 4,
        in_specs=[SMEM, SMEM, SMEM, ANY],
        out_specs=[VMEM] * 4,
        scratch_shapes=[
            pltpu.SMEM((4, rows // BLK), jnp.int32),
            pltpu.SemaphoreType.DMA((8, most)),
        ],
        compiler_params=room(12),
        name="pack_factors",
    )(large, live, pairs, factors)
    bases = pl.pallas_call(
        base_kernel,
        out_shape=[jax.ShapeDtypeStruct((rows, width), jnp.float32)] * V_PARTS,
        in_specs=[VMEM, VMEM],
        out_specs=[VMEM] * V_PARTS,
        compiler_params=room(4),
        name="base",
    )(gap, trial)
    mine = [after(side(own, got), *packed) for own, got in zip(owns, firsts)]
    theirs = [lax.ppermute(held_here, "pair", step[1]) for held_here, step in zip(mine, steps)]
    theirs[1] = after(theirs[1], *bases)

    totals, aways = [None] * V_PARTS, [None] * V_PARTS
    partial = None
    for part in reversed(range(V_PARTS)):
        own_factors, other_factors = packed[2 * part : 2 * part + 2]
        got = theirs[part] if partial is None else after(theirs[part], partial)
        partial = contract_rows(mine[part], own_factors) + contract_rows(got, other_factors)
        coeffs = exchange_sum(partial, n_aux)

        def share(of):
            return lax.dot_general(
                of, coeffs, (((1,), (1,)), ((), ())), preferred_element_type=jnp.float32
            )

        got = lax.ppermute(share(other_factors).astype(jnp.bfloat16), "pair", steps[part][1])
        totals[part] = total = share(own_factors) + got.astype(jnp.float32)
        for_small = total[cut:]
        if most > rest:
            for_small = jnp.pad(for_small, ((0, 2 * cut - held), (0, 0)))
        aways[part] = jnp.where(is_large, for_small, total[:cut]).astype(jnp.bfloat16)
    aways[0] = after(aways[0], aways[1])
    lasts = [lax.ppermute(away, "pair", step[0]) for away, step in zip(aways, steps)]
    return pl.pallas_call(
        functools.partial(finish_kernel, most),
        out_shape=jax.ShapeDtypeStruct((rows, vecs), trial.dtype),
        in_specs=[SMEM, SMEM] + [VMEM] * (3 * V_PARTS),
        out_specs=VMEM,
        compiler_params=room(6),
        name="finish",
    )(large, live, *bases, *totals, *lasts)


def on_four(n_aux, factors, trial, energy_gap, block_live):
    rows, vecs = trial.shape
    blocks = rows // BLK
    classes = [pair for pair in ((6, 3), (6, 4), (7, 4)) if max(pair) < blocks] + [(blocks, blocks)]
    at = jnp.stack([lax.axis_index("pair"), lax.axis_index("aux")]).astype(jnp.int32)
    flags = [block_live] + [
        lax.ppermute(block_live, "pair", [(z, z ^ flip) for z in range(4)]) for flip in range(1, 4)
    ]
    live, pairs, which, large, *owns = pl.pallas_call(
        functools.partial(plan_kernel, classes),
        out_shape=[
            jax.ShapeDtypeStruct((4, blocks), jnp.int32),
            jax.ShapeDtypeStruct((4,), jnp.int32),
            jax.ShapeDtypeStruct((1,), jnp.int32),
            jax.ShapeDtypeStruct((1,), jnp.int32),
        ]
        + [jax.ShapeDtypeStruct((rows, vecs // V_PARTS), trial.dtype)] * V_PARTS,
        in_specs=[SMEM] * 5 + [VMEM],
        out_specs=[SMEM] * 4 + [VMEM] * V_PARTS,
        compiler_params=room(4),
        name="plan",
    )(at, *flags, trial)
    return lax.switch(
        which[0],
        [functools.partial(along_line, *pair, n_aux) for pair in classes],
        large,
        live,
        pairs,
        trial,
        energy_gap.reshape(blocks, BLK),
        factors,
        owns,
    )


def gathered(masked, factors, n_aux):
    everyone = lax.all_gather(masked, "pair", axis=0, tiled=True)
    rows = factors.reshape(-1, factors.shape[2])
    coeffs = exchange_sum(contract_rows(everyone, rows), n_aux)
    shares = lax.dot_general(
        rows, coeffs, (((1,), (1,)), ((), ())), preferred_element_type=jnp.float32
    )
    return lax.psum_scatter(
        shares.astype(jnp.bfloat16), "pair", scatter_dimension=0, tiled=True
    ).astype(jnp.float32)


def body(n_pair, n_aux, b_built, trial, energy_gap, block_live):
    blocks = trial.shape[0] // BLK
    aux = lax.axis_index("aux")
    if n_pair == 4:
        return on_four(n_aux, b_built[0], trial, energy_gap, block_live)
    own_blocks = lax.dynamic_slice_in_dim(block_live, aux * blocks, blocks, 0)
    own_live = jnp.repeat(own_blocks, BLK)
    masked = trial * own_live.astype(jnp.bfloat16)[:, None]
    response = gathered(masked, b_built[0], n_aux)
    base = energy_gap[:, None] * trial.astype(jnp.float32)
    return (base + 2.0 * own_live.astype(jnp.float32)[:, None] * response).astype(jnp.bfloat16)


def solution(mesh):
    sizes = [mesh.shape[axis] for axis in ("pair", "aux")]
    return jax.shard_map(
        functools.partial(body, *sizes),
        mesh=mesh,
        in_specs=(
            P(("traj", "aux"), None, None, "pair"),
            P(("traj", "pair", "aux"), "root"),
            P(("traj", "pair", "aux")),
            P(("traj", "pair")),
        ),
        out_specs=P(("traj", "pair", "aux"), "root"),
        check_vma=False,
    )
```

```python
import functools

import jax
import jax.numpy as jnp
from jax import lax
from jax.experimental import pallas as pl
from jax.experimental.pallas import tpu as pltpu
from jax.sharding import PartitionSpec as P

BLK = 128
V_PARTS = 2

SMEM = pl.BlockSpec(memory_space=pltpu.SMEM)
VMEM = pl.BlockSpec(memory_space=pltpu.VMEM)
ANY = pl.BlockSpec(memory_space=pl.ANY)


def contract_rows(left, right):
    return lax.dot_general(
        left, right, (((0,), (0,)), ((), ())), preferred_element_type=jnp.float32
    )


def exchange_sum(partial, n_aux):
    sent = partial.astype(jnp.bfloat16)
    if n_aux == 1:
        return sent
    if n_aux == 2:
        other = lax.ppermute(sent, "aux", [(0, 1), (1, 0)])
        return (partial + other.astype(jnp.float32)).astype(jnp.bfloat16)
    return lax.psum(sent, "aux")


def block_rows(block):
    return pl.ds(pl.multiple_of(block * BLK, BLK), BLK)


def pack_trial_kernel(at_ref, live_ref, trial_ref, *out_refs):
    width = out_refs[0].shape[1]
    for out in out_refs:
        out[...] = jnp.zeros_like(out)
    slot = jnp.int32(0)
    blocks = trial_ref.shape[0] // BLK
    for block in range(blocks):
        here = live_ref[at_ref[1] * blocks + block]

        @pl.when(here > 0)
        def _(slot=slot, block=block):
            for part, out in enumerate(out_refs):
                out[block_rows(slot), :] = trial_ref[
                    pl.ds(block * BLK, BLK), pl.ds(part * width, width)
                ]

        slot = slot + here


def plan_kernel(classes, at_ref, own_ref, near_ref, far_ref, opposite_ref, live_ref, pairs_ref, which_ref, large_ref):
    blocks = live_ref.shape[1]
    me = at_ref[0]

    def most(ref):
        top = jnp.int32(0)
        for group in range(ref.shape[0] // blocks):
            count = ref[group * blocks]
            for block in range(1, blocks):
                count = count + ref[group * blocks + block]
            top = jnp.maximum(top, count)
        return top

    alike = jnp.maximum(most(own_ref), most(opposite_ref))
    unlike = jnp.maximum(most(near_ref), most(far_ref))
    end = (me == 0) | (me == 3)
    ends_large = jnp.where(end, alike, unlike) >= jnp.where(end, unlike, alike)
    large = end == ends_large
    large_ref[0] = large.astype(jnp.int32)
    top, other = jnp.maximum(alike, unlike), jnp.minimum(alike, unlike)
    which = jnp.int32(len(classes) - 1)
    for at in range(len(classes) - 2, -1, -1):
        which = jnp.where((top <= classes[at][0]) & (other <= classes[at][1]), at, which)
    which_ref[0] = which
    rows = (((own_ref, 0), (far_ref, 2)), ((far_ref, 2), (own_ref, 0)), ((opposite_ref, 3), (near_ref, 1)), ((near_ref, 1), (opposite_ref, 3)))
    for row, ((if_large, large_flip), (if_small, small_flip)) in enumerate(rows):
        pairs_ref[row] = me ^ jnp.where(large, large_flip, small_flip)
        for block in range(blocks):
            at = at_ref[1] * blocks + block
            live_ref[row, block] = jnp.where(large, if_large[at], if_small[at])


def pack_factors_kernel(most, rest, large_ref, live_ref, pairs_ref, factors_ref, *refs):
    outs, (index_ref, sems) = refs[:4], refs[4:]
    blocks = live_ref.shape[1]
    for row in range(4):
        for slot in range(blocks):
            index_ref[row, slot] = 0
        at = jnp.int32(0)
        for block in range(blocks):
            index_ref[row, at] = block
            at = at + live_ref[row, block]
    large = large_ref[0]
    turned = 2 * (1 - large)
    rows = ((0, 1), (2, 3), (turned, 3 - turned), (2 - turned, 1 + turned))
    copies = []
    for at, (out, pieces) in enumerate(zip(outs, rows)):
        for piece, (row, start, slots) in enumerate(zip(pieces, (0, most), (most, rest))):
            for slot in range(slots):
                copies.append(
                    pltpu.make_async_copy(
                        factors_ref.at[pairs_ref[row], block_rows(index_ref[row, slot]), :],
                        out.at[pl.ds((start + slot) * BLK, BLK), :],
                        sems.at[2 * at + piece, slot],
                    )
                )
                copies[-1].start()
    for copy in copies:
        copy.wait()


def base_kernel(gap_ref, trial_ref, *out_refs):
    width = out_refs[0].shape[1]
    for block in range(trial_ref.shape[0] // BLK):
        rows = pl.ds(block * BLK, BLK)
        gap = jnp.transpose(jnp.broadcast_to(gap_ref[pl.ds(block, 1), :], (width, BLK)))
        for part, out in enumerate(out_refs):
            out[rows, :] = gap * trial_ref[rows, pl.ds(part * width, width)].astype(jnp.float32)


def finish_kernel(most, large_ref, live_ref, *refs):
    parts = len(refs) // 3
    bases, totals, lasts, out_ref = refs[:parts], refs[parts : 2 * parts], refs[2 * parts : 3 * parts], refs[-1]
    width = out_ref.shape[1] // parts
    large = large_ref[0]
    start = (1 - large) * most
    slot = jnp.int32(0)
    for block in range(out_ref.shape[0] // BLK):
        rows = pl.ds(block * BLK, BLK)
        here = jnp.where(large > 0, live_ref[0, block], live_ref[1, block])

        @pl.when(here > 0)
        def _(slot=slot, rows=rows):
            for part in range(parts):
                last = lasts[part][block_rows(slot), :].astype(jnp.float32)
                response = totals[part][block_rows(start + slot), :] + last
                out_ref[rows, pl.ds(part * width, width)] = (
                    bases[part][rows, :] + 2.0 * response
                ).astype(out_ref.dtype)

        @pl.when(here == 0)
        def _(rows=rows):
            for part in range(parts):
                out_ref[rows, pl.ds(part * width, width)] = bases[part][rows, :].astype(out_ref.dtype)

        slot = slot + here


NEAR = [(z, z ^ 1) for z in range(4)]
FAR = [(z, z ^ 2) for z in range(4)]


def room(mebibytes):
    return pltpu.CompilerParams(vmem_limit_bytes=mebibytes * 2**20)


def after(value, *others):
    return lax.optimization_barrier((value, *others))[0]


def along_line(most, rest, n_aux, large, live, pairs, trial, gap, factors, owns):
    rows, vecs = trial.shape
    width = vecs // V_PARTS
    is_large = large[0] > 0
    cut = most * BLK
    held = cut + rest * BLK
    owns = [own[:cut] for own in owns]
    steps = ((FAR, NEAR), (NEAR, FAR))

    def side(own, got):
        return jnp.concatenate(
            [jnp.where(is_large, own, got), jnp.where(is_large, got, own)[: held - cut]]
        )

    firsts = [lax.ppermute(own, "pair", step[0]) for own, step in zip(owns, steps)]
    packed = pl.pallas_call(
        functools.partial(pack_factors_kernel, most, rest),
        out_shape=[jax.ShapeDtypeStruct((held, factors.shape[2]), factors.dtype)] * 4,
        in_specs=[SMEM, SMEM, SMEM, ANY],
        out_specs=[VMEM] * 4,
        scratch_shapes=[
            pltpu.SMEM((4, rows // BLK), jnp.int32),
            pltpu.SemaphoreType.DMA((8, most)),
        ],
        compiler_params=room(12),
        name="pack_factors",
    )(large, live, pairs, factors)
    mine = [after(side(own, got), *packed) for own, got in zip(owns, firsts)]
    bases = pl.pallas_call(
        base_kernel,
        out_shape=[jax.ShapeDtypeStruct((rows, width), jnp.float32)] * V_PARTS,
        in_specs=[VMEM, VMEM],
        out_specs=[VMEM] * V_PARTS,
        compiler_params=room(4),
        name="base",
    )(after(gap, mine[0]), trial)
    mine[1] = after(mine[1], *bases)
    theirs = [lax.ppermute(held_here, "pair", step[1]) for held_here, step in zip(mine, steps)]

    totals, aways = [None] * V_PARTS, [None] * V_PARTS
    partial = None
    for part in reversed(range(V_PARTS)):
        own_factors, other_factors = packed[2 * part : 2 * part + 2]
        got = theirs[part] if partial is None else after(theirs[part], partial)
        partial = contract_rows(mine[part], own_factors) + contract_rows(got, other_factors)
        coeffs = exchange_sum(partial, n_aux)

        def share(of):
            return lax.dot_general(
                of, coeffs, (((1,), (1,)), ((), ())), preferred_element_type=jnp.float32
            )

        got = lax.ppermute(share(other_factors).astype(jnp.bfloat16), "pair", steps[part][1])
        totals[part] = total = share(own_factors) + got.astype(jnp.float32)
        for_small = total[cut:]
        if most > rest:
            for_small = jnp.pad(for_small, ((0, 2 * cut - held), (0, 0)))
        aways[part] = jnp.where(is_large, for_small, total[:cut]).astype(jnp.bfloat16)
    aways[0] = after(aways[0], aways[1])
    lasts = [lax.ppermute(away, "pair", step[0]) for away, step in zip(aways, steps)]
    return pl.pallas_call(
        functools.partial(finish_kernel, most),
        out_shape=jax.ShapeDtypeStruct((rows, vecs), trial.dtype),
        grid=(1,),
        in_specs=[SMEM, SMEM] + [VMEM] * (3 * V_PARTS),
        out_specs=pl.BlockSpec((rows, vecs), lambda _: (0, 0)),
        compiler_params=room(6),
        name="finish",
    )(large, live, *bases, *totals, *lasts)


def on_four(n_aux, factors, trial, energy_gap, block_live):
    rows, vecs = trial.shape
    blocks = rows // BLK
    classes = [pair for pair in ((6, 3), (6, 4), (7, 4)) if max(pair) < blocks] + [(blocks, blocks)]
    at = jnp.stack([lax.axis_index("pair"), lax.axis_index("aux")]).astype(jnp.int32)
    flags = [block_live] + [
        lax.ppermute(block_live, "pair", [(z, z ^ flip) for z in range(4)]) for flip in range(1, 4)
    ]
    owns = pl.pallas_call(
        pack_trial_kernel,
        out_shape=[jax.ShapeDtypeStruct((rows, vecs // V_PARTS), trial.dtype)] * V_PARTS,
        in_specs=[SMEM, SMEM, VMEM],
        out_specs=[VMEM] * V_PARTS,
        compiler_params=room(4),
        name="pack_trial",
    )(at, block_live, trial)
    live, pairs, which, large = pl.pallas_call(
        functools.partial(plan_kernel, classes),
        out_shape=[
            jax.ShapeDtypeStruct((4, blocks), jnp.int32),
            jax.ShapeDtypeStruct((4,), jnp.int32),
            jax.ShapeDtypeStruct((1,), jnp.int32),
            jax.ShapeDtypeStruct((1,), jnp.int32),
        ],
        in_specs=[SMEM] * 5,
        out_specs=[SMEM] * 4,
        compiler_params=room(2),
        name="plan",
    )(at, *flags)
    return lax.switch(
        which[0],
        [functools.partial(along_line, *pair, n_aux) for pair in classes],
        large,
        live,
        pairs,
        trial,
        energy_gap.reshape(blocks, BLK),
        factors,
        owns,
    )


def gathered(masked, factors, n_aux):
    everyone = lax.all_gather(masked, "pair", axis=0, tiled=True)
    rows = factors.reshape(-1, factors.shape[2])
    coeffs = exchange_sum(contract_rows(everyone, rows), n_aux)
    shares = lax.dot_general(
        rows, coeffs, (((1,), (1,)), ((), ())), preferred_element_type=jnp.float32
    )
    return lax.psum_scatter(
        shares.astype(jnp.bfloat16), "pair", scatter_dimension=0, tiled=True
    ).astype(jnp.float32)


def body(n_pair, n_aux, b_built, trial, energy_gap, block_live):
    blocks = trial.shape[0] // BLK
    aux = lax.axis_index("aux")
    if n_pair == 4:
        return on_four(n_aux, b_built[0], trial, energy_gap, block_live)
    own_blocks = lax.dynamic_slice_in_dim(block_live, aux * blocks, blocks, 0)
    own_live = jnp.repeat(own_blocks, BLK)
    masked = trial * own_live.astype(jnp.bfloat16)[:, None]
    response = gathered(masked, b_built[0], n_aux)
    base = energy_gap[:, None] * trial.astype(jnp.float32)
    return (base + 2.0 * own_live.astype(jnp.float32)[:, None] * response).astype(jnp.bfloat16)


def solution(mesh):
    sizes = [mesh.shape[axis] for axis in ("pair", "aux")]
    return jax.shard_map(
        functools.partial(body, *sizes),
        mesh=mesh,
        in_specs=(
            P(("traj", "aux"), None, None, "pair"),
            P(("traj", "pair", "aux"), "root"),
            P(("traj", "pair", "aux")),
            P(("traj", "pair")),
        ),
        out_specs=P(("traj", "pair", "aux"), "root"),
        check_vma=False,
    )
```

```python
import functools

import jax
import jax.numpy as jnp
from jax import lax
from jax.experimental import pallas as pl
from jax.experimental.pallas import tpu as pltpu
from jax.sharding import PartitionSpec as P

BLK = 128
V_PARTS = 2

SMEM = pl.BlockSpec(memory_space=pltpu.SMEM)
VMEM = pl.BlockSpec(memory_space=pltpu.VMEM)
ANY = pl.BlockSpec(memory_space=pl.ANY)


def contract_rows(left, right):
    return lax.dot_general(
        left, right, (((0,), (0,)), ((), ())), preferred_element_type=jnp.float32
    )


def exchange_sum(partial, n_aux):
    sent = partial.astype(jnp.bfloat16)
    if n_aux == 1:
        return sent
    if n_aux == 2:
        other = lax.ppermute(sent, "aux", [(0, 1), (1, 0)])
        return (partial + other.astype(jnp.float32)).astype(jnp.bfloat16)
    return lax.psum(sent, "aux")


def block_rows(block):
    return pl.ds(pl.multiple_of(block * BLK, BLK), BLK)


def pack_trial_kernel(at_ref, live_ref, trial_ref, *out_refs):
    width = out_refs[0].shape[1]
    for out in out_refs:
        out[...] = jnp.zeros_like(out)
    slot = jnp.int32(0)
    blocks = trial_ref.shape[0] // BLK
    for block in range(blocks):
        here = live_ref[at_ref[1] * blocks + block]

        @pl.when(here > 0)
        def _(slot=slot, block=block):
            for part, out in enumerate(out_refs):
                out[block_rows(slot), :] = trial_ref[
                    pl.ds(block * BLK, BLK), pl.ds(part * width, width)
                ]

        slot = slot + here


def plan_kernel(classes, at_ref, own_ref, near_ref, far_ref, opposite_ref, live_ref, pairs_ref, which_ref, large_ref):
    blocks = live_ref.shape[1]
    me = at_ref[0]

    def most(ref):
        top = jnp.int32(0)
        for group in range(ref.shape[0] // blocks):
            count = ref[group * blocks]
            for block in range(1, blocks):
                count = count + ref[group * blocks + block]
            top = jnp.maximum(top, count)
        return top

    alike = jnp.maximum(most(own_ref), most(opposite_ref))
    unlike = jnp.maximum(most(near_ref), most(far_ref))
    end = (me == 0) | (me == 3)
    ends_large = jnp.where(end, alike, unlike) >= jnp.where(end, unlike, alike)
    large = end == ends_large
    large_ref[0] = large.astype(jnp.int32)
    top, other = jnp.maximum(alike, unlike), jnp.minimum(alike, unlike)
    which = jnp.int32(len(classes) - 1)
    for at in range(len(classes) - 2, -1, -1):
        which = jnp.where((top <= classes[at][0]) & (other <= classes[at][1]), at, which)
    which_ref[0] = which
    rows = (((own_ref, 0), (far_ref, 2)), ((far_ref, 2), (own_ref, 0)), ((opposite_ref, 3), (near_ref, 1)), ((near_ref, 1), (opposite_ref, 3)))
    for row, ((if_large, large_flip), (if_small, small_flip)) in enumerate(rows):
        pairs_ref[row] = me ^ jnp.where(large, large_flip, small_flip)
        for block in range(blocks):
            at = at_ref[1] * blocks + block
            live_ref[row, block] = jnp.where(large, if_large[at], if_small[at])


def pack_factors_kernel(most, rest, large_ref, live_ref, pairs_ref, factors_ref, *refs):
    outs, (index_ref, sems) = refs[:4], refs[4:]
    blocks = live_ref.shape[1]
    for row in range(4):
        for slot in range(blocks):
            index_ref[row, slot] = 0
        at = jnp.int32(0)
        for block in range(blocks):
            index_ref[row, at] = block
            at = at + live_ref[row, block]
    large = large_ref[0]
    turned = 2 * (1 - large)
    rows = ((0, 1), (2, 3), (turned, 3 - turned), (2 - turned, 1 + turned))
    copies = []
    for at, (out, pieces) in enumerate(zip(outs, rows)):
        for piece, (row, start, slots) in enumerate(zip(pieces, (0, most), (most, rest))):
            for slot in range(slots):
                copies.append(
                    pltpu.make_async_copy(
                        factors_ref.at[pairs_ref[row], block_rows(index_ref[row, slot]), :],
                        out.at[pl.ds((start + slot) * BLK, BLK), :],
                        sems.at[2 * at + piece, slot],
                    )
                )
                copies[-1].start()
    for copy in copies:
        copy.wait()


def base_kernel(gap_ref, trial_ref, *out_refs):
    width = out_refs[0].shape[1]
    for block in range(trial_ref.shape[0] // BLK):
        rows = pl.ds(block * BLK, BLK)
        gap = jnp.transpose(jnp.broadcast_to(gap_ref[pl.ds(block, 1), :], (width, BLK)))
        for part, out in enumerate(out_refs):
            out[rows, :] = gap * trial_ref[rows, pl.ds(part * width, width)].astype(jnp.float32)


def finish_kernel(most, parts, large_ref, live_ref, *refs):
    bases, totals, lasts = refs[:parts], refs[parts : 2 * parts], refs[2 * parts : 3 * parts]
    out_ref, held_ref, sems = refs[3 * parts :]
    width = held_ref.shape[1] // parts
    large = large_ref[0]
    start = (1 - large) * most
    slot = jnp.int32(0)
    copies = []
    for block in range(held_ref.shape[0] // BLK):
        rows = pl.ds(block * BLK, BLK)
        here = jnp.where(large > 0, live_ref[0, block], live_ref[1, block])

        @pl.when(here > 0)
        def _(slot=slot, rows=rows):
            for part in range(parts):
                last = lasts[part][block_rows(slot), :].astype(jnp.float32)
                response = totals[part][block_rows(start + slot), :] + last
                held_ref[rows, pl.ds(part * width, width)] = (
                    bases[part][rows, :] + 2.0 * response
                ).astype(held_ref.dtype)

        @pl.when(here == 0)
        def _(rows=rows):
            for part in range(parts):
                held_ref[rows, pl.ds(part * width, width)] = bases[part][rows, :].astype(held_ref.dtype)

        copies.append(
            pltpu.make_async_copy(held_ref.at[rows, :], out_ref.at[rows, :], sems.at[block])
        )
        copies[-1].start()
        slot = slot + here
    for copy in copies:
        copy.wait()


NEAR = [(z, z ^ 1) for z in range(4)]
FAR = [(z, z ^ 2) for z in range(4)]


def room(mebibytes):
    return pltpu.CompilerParams(vmem_limit_bytes=mebibytes * 2**20)


def after(value, *others):
    return lax.optimization_barrier((value, *others))[0]


def along_line(most, rest, n_aux, large, live, pairs, trial, gap, factors, owns):
    rows, vecs = trial.shape
    width = vecs // V_PARTS
    is_large = large[0] > 0
    cut = most * BLK
    held = cut + rest * BLK
    owns = [own[:cut] for own in owns]
    steps = ((FAR, NEAR), (NEAR, FAR))

    def side(own, got):
        return jnp.concatenate(
            [jnp.where(is_large, own, got), jnp.where(is_large, got, own)[: held - cut]]
        )

    firsts = [lax.ppermute(own, "pair", step[0]) for own, step in zip(owns, steps)]
    packed = pl.pallas_call(
        functools.partial(pack_factors_kernel, most, rest),
        out_shape=[jax.ShapeDtypeStruct((held, factors.shape[2]), factors.dtype)] * 4,
        in_specs=[SMEM, SMEM, SMEM, ANY],
        out_specs=[VMEM] * 4,
        scratch_shapes=[
            pltpu.SMEM((4, rows // BLK), jnp.int32),
            pltpu.SemaphoreType.DMA((8, most)),
        ],
        compiler_params=room(12),
        name="pack_factors",
    )(large, live, pairs, factors)
    bases = pl.pallas_call(
        base_kernel,
        out_shape=[jax.ShapeDtypeStruct((rows, width), jnp.float32)] * V_PARTS,
        in_specs=[VMEM, VMEM],
        out_specs=[VMEM] * V_PARTS,
        compiler_params=room(4),
        name="base",
    )(gap, trial)
    mine = [after(side(own, got), *packed) for own, got in zip(owns, firsts)]
    theirs = [lax.ppermute(held_here, "pair", step[1]) for held_here, step in zip(mine, steps)]
    theirs[1] = after(theirs[1], *bases)

    totals, aways = [None] * V_PARTS, [None] * V_PARTS
    partial = None
    for part in reversed(range(V_PARTS)):
        own_factors, other_factors = packed[2 * part : 2 * part + 2]
        got = theirs[part] if partial is None else after(theirs[part], partial)
        partial = contract_rows(mine[part], own_factors) + contract_rows(got, other_factors)
        coeffs = exchange_sum(partial, n_aux)

        def share(of):
            return lax.dot_general(
                of, coeffs, (((1,), (1,)), ((), ())), preferred_element_type=jnp.float32
            )

        got = lax.ppermute(share(other_factors).astype(jnp.bfloat16), "pair", steps[part][1])
        totals[part] = total = share(own_factors) + got.astype(jnp.float32)
        for_small = total[cut:]
        if most > rest:
            for_small = jnp.pad(for_small, ((0, 2 * cut - held), (0, 0)))
        aways[part] = jnp.where(is_large, for_small, total[:cut]).astype(jnp.bfloat16)
    aways[0] = after(aways[0], aways[1])
    lasts = [lax.ppermute(away, "pair", step[0]) for away, step in zip(aways, steps)]
    return pl.pallas_call(
        functools.partial(finish_kernel, most, V_PARTS),
        out_shape=jax.ShapeDtypeStruct((rows, vecs), trial.dtype),
        in_specs=[SMEM, SMEM] + [VMEM] * (3 * V_PARTS),
        out_specs=pl.BlockSpec(memory_space=pltpu.HBM),
        scratch_shapes=[
            pltpu.VMEM((rows, vecs), trial.dtype),
            pltpu.SemaphoreType.DMA((rows // BLK,)),
        ],
        compiler_params=room(6),
        name="finish",
    )(large, live, *bases, *totals, *lasts)


def on_four(n_aux, factors, trial, energy_gap, block_live):
    rows, vecs = trial.shape
    blocks = rows // BLK
    classes = [pair for pair in ((6, 3), (6, 4), (7, 4)) if max(pair) < blocks] + [(blocks, blocks)]
    at = jnp.stack([lax.axis_index("pair"), lax.axis_index("aux")]).astype(jnp.int32)
    flags = [block_live] + [
        lax.ppermute(block_live, "pair", [(z, z ^ flip) for z in range(4)]) for flip in range(1, 4)
    ]
    owns = pl.pallas_call(
        pack_trial_kernel,
        out_shape=[jax.ShapeDtypeStruct((rows, vecs // V_PARTS), trial.dtype)] * V_PARTS,
        in_specs=[SMEM, SMEM, VMEM],
        out_specs=[VMEM] * V_PARTS,
        compiler_params=room(4),
        name="pack_trial",
    )(at, block_live, trial)
    live, pairs, which, large = pl.pallas_call(
        functools.partial(plan_kernel, classes),
        out_shape=[
            jax.ShapeDtypeStruct((4, blocks), jnp.int32),
            jax.ShapeDtypeStruct((4,), jnp.int32),
            jax.ShapeDtypeStruct((1,), jnp.int32),
            jax.ShapeDtypeStruct((1,), jnp.int32),
        ],
        in_specs=[SMEM] * 5,
        out_specs=[SMEM] * 4,
        compiler_params=room(2),
        name="plan",
    )(at, *flags)
    return lax.switch(
        which[0],
        [functools.partial(along_line, *pair, n_aux) for pair in classes],
        large,
        live,
        pairs,
        trial,
        energy_gap.reshape(blocks, BLK),
        factors,
        owns,
    )


def gathered(masked, factors, n_aux):
    everyone = lax.all_gather(masked, "pair", axis=0, tiled=True)
    rows = factors.reshape(-1, factors.shape[2])
    coeffs = exchange_sum(contract_rows(everyone, rows), n_aux)
    shares = lax.dot_general(
        rows, coeffs, (((1,), (1,)), ((), ())), preferred_element_type=jnp.float32
    )
    return lax.psum_scatter(
        shares.astype(jnp.bfloat16), "pair", scatter_dimension=0, tiled=True
    ).astype(jnp.float32)


def body(n_pair, n_aux, b_built, trial, energy_gap, block_live):
    blocks = trial.shape[0] // BLK
    aux = lax.axis_index("aux")
    if n_pair == 4:
        return on_four(n_aux, b_built[0], trial, energy_gap, block_live)
    own_blocks = lax.dynamic_slice_in_dim(block_live, aux * blocks, blocks, 0)
    own_live = jnp.repeat(own_blocks, BLK)
    masked = trial * own_live.astype(jnp.bfloat16)[:, None]
    response = gathered(masked, b_built[0], n_aux)
    base = energy_gap[:, None] * trial.astype(jnp.float32)
    return (base + 2.0 * own_live.astype(jnp.float32)[:, None] * response).astype(jnp.bfloat16)


def solution(mesh):
    sizes = [mesh.shape[axis] for axis in ("pair", "aux")]
    return jax.shard_map(
        functools.partial(body, *sizes),
        mesh=mesh,
        in_specs=(
            P(("traj", "aux"), None, None, "pair"),
            P(("traj", "pair", "aux"), "root"),
            P(("traj", "pair", "aux")),
            P(("traj", "pair")),
        ),
        out_specs=P(("traj", "pair", "aux"), "root"),
        check_vma=False,
    )
```

```python
import functools

import jax
import jax.numpy as jnp
from jax import lax
from jax.experimental import pallas as pl
from jax.experimental.pallas import tpu as pltpu
from jax.sharding import PartitionSpec as P

BLK = 128
V_PARTS = 2

SMEM = pl.BlockSpec(memory_space=pltpu.SMEM)
VMEM = pl.BlockSpec(memory_space=pltpu.VMEM)
ANY = pl.BlockSpec(memory_space=pl.ANY)


def contract_rows(left, right):
    return lax.dot_general(
        left, right, (((0,), (0,)), ((), ())), preferred_element_type=jnp.float32
    )


def exchange_sum(partial, n_aux):
    sent = partial.astype(jnp.bfloat16)
    if n_aux == 1:
        return sent
    if n_aux == 2:
        other = lax.ppermute(sent, "aux", [(0, 1), (1, 0)])
        return (partial + other.astype(jnp.float32)).astype(jnp.bfloat16)
    return lax.psum(sent, "aux")


def block_rows(block):
    return pl.ds(pl.multiple_of(block * BLK, BLK), BLK)


def pack_trial_kernel(at_ref, live_ref, trial_ref, *out_refs):
    width = out_refs[0].shape[1]
    for out in out_refs:
        out[...] = jnp.zeros_like(out)
    slot = jnp.int32(0)
    blocks = trial_ref.shape[0] // BLK
    for block in range(blocks):
        here = live_ref[at_ref[1] * blocks + block]

        @pl.when(here > 0)
        def _(slot=slot, block=block):
            for part, out in enumerate(out_refs):
                out[block_rows(slot), :] = trial_ref[
                    pl.ds(block * BLK, BLK), pl.ds(part * width, width)
                ]

        slot = slot + here


def plan_kernel(classes, at_ref, own_ref, near_ref, far_ref, opposite_ref, live_ref, pairs_ref, which_ref, large_ref):
    blocks = live_ref.shape[1]
    me = at_ref[0]

    def most(ref):
        top = jnp.int32(0)
        for group in range(ref.shape[0] // blocks):
            count = ref[group * blocks]
            for block in range(1, blocks):
                count = count + ref[group * blocks + block]
            top = jnp.maximum(top, count)
        return top

    alike = jnp.maximum(most(own_ref), most(opposite_ref))
    unlike = jnp.maximum(most(near_ref), most(far_ref))
    end = (me == 0) | (me == 3)
    ends_large = jnp.where(end, alike, unlike) >= jnp.where(end, unlike, alike)
    large = end == ends_large
    large_ref[0] = large.astype(jnp.int32)
    top, other = jnp.maximum(alike, unlike), jnp.minimum(alike, unlike)
    which = jnp.int32(len(classes) - 1)
    for at in range(len(classes) - 2, -1, -1):
        which = jnp.where((top <= classes[at][0]) & (other <= classes[at][1]), at, which)
    which_ref[0] = which
    rows = (((own_ref, 0), (far_ref, 2)), ((far_ref, 2), (own_ref, 0)), ((opposite_ref, 3), (near_ref, 1)), ((near_ref, 1), (opposite_ref, 3)))
    for row, ((if_large, large_flip), (if_small, small_flip)) in enumerate(rows):
        pairs_ref[row] = me ^ jnp.where(large, large_flip, small_flip)
        for block in range(blocks):
            at = at_ref[1] * blocks + block
            live_ref[row, block] = jnp.where(large, if_large[at], if_small[at])


def pack_factors_kernel(most, rest, large_ref, live_ref, pairs_ref, factors_ref, *refs):
    outs, (index_ref, sems) = refs[:4], refs[4:]
    blocks = live_ref.shape[1]
    for row in range(4):
        for slot in range(blocks):
            index_ref[row, slot] = 0
        at = jnp.int32(0)
        for block in range(blocks):
            index_ref[row, at] = block
            at = at + live_ref[row, block]
    large = large_ref[0]
    turned = 2 * (1 - large)
    rows = ((0, 1), (2, 3), (turned, 3 - turned), (2 - turned, 1 + turned))
    copies = []
    for at, (out, pieces) in enumerate(zip(outs, rows)):
        for piece, (row, start, slots) in enumerate(zip(pieces, (0, most), (most, rest))):
            for slot in range(slots):
                copies.append(
                    pltpu.make_async_copy(
                        factors_ref.at[pairs_ref[row], block_rows(index_ref[row, slot]), :],
                        out.at[pl.ds((start + slot) * BLK, BLK), :],
                        sems.at[2 * at + piece, slot],
                    )
                )
                copies[-1].start()
    for copy in copies:
        copy.wait()


def base_kernel(gap_ref, trial_ref, *out_refs):
    width = out_refs[0].shape[1]
    for block in range(trial_ref.shape[0] // BLK):
        rows = pl.ds(block * BLK, BLK)
        gap = jnp.transpose(jnp.broadcast_to(gap_ref[pl.ds(block, 1), :], (width, BLK)))
        for part, out in enumerate(out_refs):
            out[rows, :] = gap * trial_ref[rows, pl.ds(part * width, width)].astype(jnp.float32)


def finish_kernel(most, large_ref, live_ref, base_ref, sum_ref, far_ref, *refs):
    out_ref = refs[-1]
    large = large_ref[0]
    start = (1 - large) * most
    slot = jnp.int32(0)
    for block in range(out_ref.shape[0] // BLK):
        rows = pl.ds(block * BLK, BLK)
        here = jnp.where(large > 0, live_ref[0, block], live_ref[1, block])

        @pl.when(here > 0)
        def _(slot=slot, rows=rows):
            response = sum_ref[block_rows(start + slot), :] + far_ref[block_rows(slot), :].astype(jnp.float32)
            out_ref[rows, :] = (base_ref[rows, :] + 2.0 * response).astype(out_ref.dtype)

        @pl.when(here == 0)
        def _(rows=rows):
            out_ref[rows, :] = base_ref[rows, :].astype(out_ref.dtype)

        slot = slot + here


NEAR = [(z, z ^ 1) for z in range(4)]
FAR = [(z, z ^ 2) for z in range(4)]


def room(mebibytes):
    return pltpu.CompilerParams(vmem_limit_bytes=mebibytes * 2**20)


def after(value, *others):
    return lax.optimization_barrier((value, *others))[0]


def along_line(most, rest, n_aux, large, live, pairs, trial, gap, factors, owns):
    rows, vecs = trial.shape
    width = vecs // V_PARTS
    is_large = large[0] > 0
    cut = most * BLK
    held = cut + rest * BLK
    owns = [own[:cut] for own in owns]
    steps = ((FAR, NEAR), (NEAR, FAR))

    def side(own, got):
        return jnp.concatenate(
            [jnp.where(is_large, own, got), jnp.where(is_large, got, own)[: held - cut]]
        )

    firsts = [lax.ppermute(own, "pair", step[0]) for own, step in zip(owns, steps)]
    packed = pl.pallas_call(
        functools.partial(pack_factors_kernel, most, rest),
        out_shape=[jax.ShapeDtypeStruct((held, factors.shape[2]), factors.dtype)] * 4,
        in_specs=[SMEM, SMEM, SMEM, ANY],
        out_specs=[VMEM] * 4,
        scratch_shapes=[
            pltpu.SMEM((4, rows // BLK), jnp.int32),
            pltpu.SemaphoreType.DMA((8, most)),
        ],
        compiler_params=room(12),
        name="pack_factors",
    )(large, live, pairs, factors)
    bases = pl.pallas_call(
        base_kernel,
        out_shape=[jax.ShapeDtypeStruct((rows, width), jnp.float32)] * V_PARTS,
        in_specs=[VMEM, VMEM],
        out_specs=[VMEM] * V_PARTS,
        compiler_params=room(4),
        name="base",
    )(gap, trial)
    mine = [after(side(own, got), *packed) for own, got in zip(owns, firsts)]
    theirs = [lax.ppermute(held_here, "pair", step[1]) for held_here, step in zip(mine, steps)]
    theirs[1] = after(theirs[1], *bases)

    totals, aways = [], []
    partial = sent = None
    for part in range(V_PARTS):
        own_factors, other_factors = packed[2 * part : 2 * part + 2]
        got = theirs[part] if partial is None else after(theirs[part], partial)
        partial = contract_rows(mine[part], own_factors) + contract_rows(got, other_factors)
        coeffs = exchange_sum(partial, n_aux)

        def share(of):
            return lax.dot_general(
                of, coeffs, (((1,), (1,)), ((), ())), preferred_element_type=jnp.float32
            )

        ready = share(other_factors).astype(jnp.bfloat16)
        sent = ready if sent is None else after(ready, sent)
        got = lax.ppermute(sent, "pair", steps[part][1])
        total = share(own_factors) + got.astype(jnp.float32)
        for_small = total[cut:]
        if most > rest:
            for_small = jnp.pad(for_small, ((0, 2 * cut - held), (0, 0)))
        totals.append(total)
        aways.append(jnp.where(is_large, for_small, total[:cut]).astype(jnp.bfloat16))
    aways[0] = after(aways[0], aways[1])
    sigma = None
    for part in reversed(range(V_PARTS)):
        got = lax.ppermute(aways[part], "pair", steps[part][0])
        begun = sigma is not None
        sigma = pl.pallas_call(
            functools.partial(finish_kernel, most),
            out_shape=jax.ShapeDtypeStruct((rows, vecs), trial.dtype),
            grid=(1,),
            in_specs=[SMEM, SMEM, VMEM, VMEM, VMEM] + ([ANY] if begun else []),
            out_specs=pl.BlockSpec((rows, width), lambda _, part=part: (0, part)),
            input_output_aliases={5: 0} if begun else {},
            compiler_params=room(6),
            name="finish",
        )(large, live, bases[part], totals[part], got, *([sigma] if begun else []))
    return sigma


def on_four(n_aux, factors, trial, energy_gap, block_live):
    rows, vecs = trial.shape
    blocks = rows // BLK
    classes = [pair for pair in ((6, 3), (6, 4), (7, 4)) if max(pair) < blocks] + [(blocks, blocks)]
    at = jnp.stack([lax.axis_index("pair"), lax.axis_index("aux")]).astype(jnp.int32)
    flags = [block_live] + [
        lax.ppermute(block_live, "pair", [(z, z ^ flip) for z in range(4)]) for flip in range(1, 4)
    ]
    owns = pl.pallas_call(
        pack_trial_kernel,
        out_shape=[jax.ShapeDtypeStruct((rows, vecs // V_PARTS), trial.dtype)] * V_PARTS,
        in_specs=[SMEM, SMEM, VMEM],
        out_specs=[VMEM] * V_PARTS,
        compiler_params=room(4),
        name="pack_trial",
    )(at, block_live, trial)
    live, pairs, which, large = pl.pallas_call(
        functools.partial(plan_kernel, classes),
        out_shape=[
            jax.ShapeDtypeStruct((4, blocks), jnp.int32),
            jax.ShapeDtypeStruct((4,), jnp.int32),
            jax.ShapeDtypeStruct((1,), jnp.int32),
            jax.ShapeDtypeStruct((1,), jnp.int32),
        ],
        in_specs=[SMEM] * 5,
        out_specs=[SMEM] * 4,
        compiler_params=room(2),
        name="plan",
    )(at, *flags)
    return lax.switch(
        which[0],
        [functools.partial(along_line, *pair, n_aux) for pair in classes],
        large,
        live,
        pairs,
        trial,
        energy_gap.reshape(blocks, BLK),
        factors,
        owns,
    )


def gathered(masked, factors, n_aux):
    everyone = lax.all_gather(masked, "pair", axis=0, tiled=True)
    rows = factors.reshape(-1, factors.shape[2])
    coeffs = exchange_sum(contract_rows(everyone, rows), n_aux)
    shares = lax.dot_general(
        rows, coeffs, (((1,), (1,)), ((), ())), preferred_element_type=jnp.float32
    )
    return lax.psum_scatter(
        shares.astype(jnp.bfloat16), "pair", scatter_dimension=0, tiled=True
    ).astype(jnp.float32)


def body(n_pair, n_aux, b_built, trial, energy_gap, block_live):
    blocks = trial.shape[0] // BLK
    aux = lax.axis_index("aux")
    if n_pair == 4:
        return on_four(n_aux, b_built[0], trial, energy_gap, block_live)
    own_blocks = lax.dynamic_slice_in_dim(block_live, aux * blocks, blocks, 0)
    own_live = jnp.repeat(own_blocks, BLK)
    masked = trial * own_live.astype(jnp.bfloat16)[:, None]
    response = gathered(masked, b_built[0], n_aux)
    base = energy_gap[:, None] * trial.astype(jnp.float32)
    return (base + 2.0 * own_live.astype(jnp.float32)[:, None] * response).astype(jnp.bfloat16)


def solution(mesh):
    sizes = [mesh.shape[axis] for axis in ("pair", "aux")]
    return jax.shard_map(
        functools.partial(body, *sizes),
        mesh=mesh,
        in_specs=(
            P(("traj", "aux"), None, None, "pair"),
            P(("traj", "pair", "aux"), "root"),
            P(("traj", "pair", "aux")),
            P(("traj", "pair")),
        ),
        out_specs=P(("traj", "pair", "aux"), "root"),
        check_vma=False,
    )
```

```python
import functools

import jax
import jax.numpy as jnp
from jax import lax
from jax.experimental import pallas as pl
from jax.experimental.pallas import tpu as pltpu
from jax.sharding import PartitionSpec as P

BLK = 128
V_PARTS = 2

SMEM = pl.BlockSpec(memory_space=pltpu.SMEM)
VMEM = pl.BlockSpec(memory_space=pltpu.VMEM)
ANY = pl.BlockSpec(memory_space=pl.ANY)


def contract_rows(left, right):
    return lax.dot_general(
        left, right, (((0,), (0,)), ((), ())), preferred_element_type=jnp.float32
    )


def exchange_sum(partial, n_aux):
    sent = partial.astype(jnp.bfloat16)
    if n_aux == 1:
        return sent
    if n_aux == 2:
        other = lax.ppermute(sent, "aux", [(0, 1), (1, 0)])
        return (partial + other.astype(jnp.float32)).astype(jnp.bfloat16)
    return lax.psum(sent, "aux")


def block_rows(block):
    return pl.ds(pl.multiple_of(block * BLK, BLK), BLK)


def pack_trial_kernel(at_ref, live_ref, trial_ref, *out_refs):
    width = out_refs[0].shape[1]
    for out in out_refs:
        out[...] = jnp.zeros_like(out)
    slot = jnp.int32(0)
    blocks = trial_ref.shape[0] // BLK
    for block in range(blocks):
        here = live_ref[at_ref[1] * blocks + block]

        @pl.when(here > 0)
        def _(slot=slot, block=block):
            for part, out in enumerate(out_refs):
                out[block_rows(slot), :] = trial_ref[
                    pl.ds(block * BLK, BLK), pl.ds(part * width, width)
                ]

        slot = slot + here


def plan_kernel(classes, at_ref, own_ref, near_ref, far_ref, opposite_ref, live_ref, pairs_ref, which_ref, large_ref):
    blocks = live_ref.shape[1]
    me = at_ref[0]

    def most(ref):
        top = jnp.int32(0)
        for group in range(ref.shape[0] // blocks):
            count = ref[group * blocks]
            for block in range(1, blocks):
                count = count + ref[group * blocks + block]
            top = jnp.maximum(top, count)
        return top

    alike = jnp.maximum(most(own_ref), most(opposite_ref))
    unlike = jnp.maximum(most(near_ref), most(far_ref))
    end = (me == 0) | (me == 3)
    ends_large = jnp.where(end, alike, unlike) >= jnp.where(end, unlike, alike)
    large = end == ends_large
    large_ref[0] = large.astype(jnp.int32)
    top, other = jnp.maximum(alike, unlike), jnp.minimum(alike, unlike)
    which = jnp.int32(len(classes) - 1)
    for at in range(len(classes) - 2, -1, -1):
        which = jnp.where((top <= classes[at][0]) & (other <= classes[at][1]), at, which)
    which_ref[0] = which
    rows = (((own_ref, 0), (far_ref, 2)), ((far_ref, 2), (own_ref, 0)), ((opposite_ref, 3), (near_ref, 1)), ((near_ref, 1), (opposite_ref, 3)))
    for row, ((if_large, large_flip), (if_small, small_flip)) in enumerate(rows):
        pairs_ref[row] = me ^ jnp.where(large, large_flip, small_flip)
        for block in range(blocks):
            at = at_ref[1] * blocks + block
            live_ref[row, block] = jnp.where(large, if_large[at], if_small[at])


def pack_factors_kernel(most, rest, large_ref, live_ref, pairs_ref, factors_ref, *refs):
    outs, (index_ref, sems) = refs[:4], refs[4:]
    blocks = live_ref.shape[1]
    for row in range(4):
        for slot in range(blocks):
            index_ref[row, slot] = 0
        at = jnp.int32(0)
        for block in range(blocks):
            index_ref[row, at] = block
            at = at + live_ref[row, block]
    large = large_ref[0]
    turned = 2 * (1 - large)
    rows = ((0, 1), (2, 3), (turned, 3 - turned), (2 - turned, 1 + turned))
    copies = []
    for at, (out, pieces) in enumerate(zip(outs, rows)):
        for piece, (row, start, slots) in enumerate(zip(pieces, (0, most), (most, rest))):
            for slot in range(slots):
                copies.append(
                    pltpu.make_async_copy(
                        factors_ref.at[pairs_ref[row], block_rows(index_ref[row, slot]), :],
                        out.at[pl.ds((start + slot) * BLK, BLK), :],
                        sems.at[2 * at + piece, slot],
                    )
                )
                copies[-1].start()
    for copy in copies:
        copy.wait()


def base_kernel(gap_ref, trial_ref, *out_refs):
    width = out_refs[0].shape[1]
    for block in range(trial_ref.shape[0] // BLK):
        rows = pl.ds(block * BLK, BLK)
        gap = jnp.transpose(jnp.broadcast_to(gap_ref[pl.ds(block, 1), :], (width, BLK)))
        for part, out in enumerate(out_refs):
            out[rows, :] = gap * trial_ref[rows, pl.ds(part * width, width)].astype(jnp.float32)


def finish_kernel(most, large_ref, live_ref, base_ref, sum_ref, far_ref, *refs):
    out_ref = refs[-1]
    large = large_ref[0]
    start = (1 - large) * most
    slot = jnp.int32(0)
    for block in range(out_ref.shape[0] // BLK):
        rows = pl.ds(block * BLK, BLK)
        here = jnp.where(large > 0, live_ref[0, block], live_ref[1, block])

        @pl.when(here > 0)
        def _(slot=slot, rows=rows):
            response = sum_ref[block_rows(start + slot), :] + far_ref[block_rows(slot), :].astype(jnp.float32)
            out_ref[rows, :] = (base_ref[rows, :] + 2.0 * response).astype(out_ref.dtype)

        @pl.when(here == 0)
        def _(rows=rows):
            out_ref[rows, :] = base_ref[rows, :].astype(out_ref.dtype)

        slot = slot + here


NEAR = [(z, z ^ 1) for z in range(4)]
FAR = [(z, z ^ 2) for z in range(4)]


def room(mebibytes):
    return pltpu.CompilerParams(vmem_limit_bytes=mebibytes * 2**20)


def after(value, *others):
    return lax.optimization_barrier((value, *others))[0]


def along_line(most, rest, n_aux, large, live, pairs, trial, gap, factors, owns):
    rows, vecs = trial.shape
    width = vecs // V_PARTS
    is_large = large[0] > 0
    cut = most * BLK
    held = cut + rest * BLK
    owns = [own[:cut] for own in owns]
    steps = ((FAR, NEAR), (NEAR, FAR))

    def side(own, got):
        return jnp.concatenate(
            [jnp.where(is_large, own, got), jnp.where(is_large, got, own)[: held - cut]]
        )

    firsts = [lax.ppermute(own, "pair", step[0]) for own, step in zip(owns, steps)]
    packed = pl.pallas_call(
        functools.partial(pack_factors_kernel, most, rest),
        out_shape=[jax.ShapeDtypeStruct((held, factors.shape[2]), factors.dtype)] * 4,
        in_specs=[SMEM, SMEM, SMEM, ANY],
        out_specs=[VMEM] * 4,
        scratch_shapes=[
            pltpu.SMEM((4, rows // BLK), jnp.int32),
            pltpu.SemaphoreType.DMA((8, most)),
        ],
        compiler_params=room(12),
        name="pack_factors",
    )(large, live, pairs, factors)
    bases = pl.pallas_call(
        base_kernel,
        out_shape=[jax.ShapeDtypeStruct((rows, width), jnp.float32)] * V_PARTS,
        in_specs=[VMEM, VMEM],
        out_specs=[VMEM] * V_PARTS,
        compiler_params=room(4),
        name="base",
    )(gap, trial)
    mine = [after(side(own, got), *packed) for own, got in zip(owns, firsts)]
    theirs = [lax.ppermute(held_here, "pair", step[1]) for held_here, step in zip(mine, steps)]
    theirs[1] = after(theirs[1], *bases)

    totals, aways = [None] * V_PARTS, [None] * V_PARTS
    partial = None
    for part in reversed(range(V_PARTS)):
        own_factors, other_factors = packed[2 * part : 2 * part + 2]
        got = theirs[part] if partial is None else after(theirs[part], partial)
        partial = contract_rows(mine[part], own_factors) + contract_rows(got, other_factors)
        coeffs = exchange_sum(partial, n_aux)

        def share(of):
            return lax.dot_general(
                of, coeffs, (((1,), (1,)), ((), ())), preferred_element_type=jnp.float32
            )

        got = lax.ppermute(share(other_factors).astype(jnp.bfloat16), "pair", steps[part][1])
        totals[part] = total = share(own_factors) + got.astype(jnp.float32)
        for_small = total[cut:]
        if most > rest:
            for_small = jnp.pad(for_small, ((0, 2 * cut - held), (0, 0)))
        aways[part] = jnp.where(is_large, for_small, total[:cut]).astype(jnp.bfloat16)
    aways[0] = after(aways[0], aways[1])
    sigma = None
    for part in reversed(range(V_PARTS)):
        got = lax.ppermute(aways[part], "pair", steps[part][0])
        begun = sigma is not None
        sigma = pl.pallas_call(
            functools.partial(finish_kernel, most),
            out_shape=jax.ShapeDtypeStruct((rows, vecs), trial.dtype),
            grid=(1,),
            in_specs=[SMEM, SMEM, VMEM, VMEM, VMEM] + ([ANY] if begun else []),
            out_specs=pl.BlockSpec((rows, width), lambda _, part=part: (0, part)),
            input_output_aliases={5: 0} if begun else {},
            compiler_params=room(6),
            name="finish",
        )(large, live, bases[part], totals[part], got, *([sigma] if begun else []))
    return sigma


def on_four(n_aux, factors, trial, energy_gap, block_live):
    rows, vecs = trial.shape
    blocks = rows // BLK
    classes = [pair for pair in ((6, 3), (6, 4), (7, 4)) if max(pair) < blocks] + [(blocks, blocks)]
    at = jnp.stack([lax.axis_index("pair"), lax.axis_index("aux")]).astype(jnp.int32)
    flags = [block_live] + [
        lax.ppermute(block_live, "pair", [(z, z ^ flip) for z in range(4)]) for flip in range(1, 4)
    ]
    owns = pl.pallas_call(
        pack_trial_kernel,
        out_shape=[jax.ShapeDtypeStruct((rows, vecs // V_PARTS), trial.dtype)] * V_PARTS,
        in_specs=[SMEM, SMEM, VMEM],
        out_specs=[VMEM] * V_PARTS,
        compiler_params=room(4),
        name="pack_trial",
    )(at, block_live, trial)
    live, pairs, which, large = pl.pallas_call(
        functools.partial(plan_kernel, classes),
        out_shape=[
            jax.ShapeDtypeStruct((4, blocks), jnp.int32),
            jax.ShapeDtypeStruct((4,), jnp.int32),
            jax.ShapeDtypeStruct((1,), jnp.int32),
            jax.ShapeDtypeStruct((1,), jnp.int32),
        ],
        in_specs=[SMEM] * 5,
        out_specs=[SMEM] * 4,
        compiler_params=room(2),
        name="plan",
    )(at, *flags)
    return lax.switch(
        which[0],
        [functools.partial(along_line, *pair, n_aux) for pair in classes],
        large,
        live,
        pairs,
        trial,
        energy_gap.reshape(blocks, BLK),
        factors,
        owns,
    )


def gathered(masked, factors, n_aux):
    everyone = lax.all_gather(masked, "pair", axis=0, tiled=True)
    rows = factors.reshape(-1, factors.shape[2])
    coeffs = exchange_sum(contract_rows(everyone, rows), n_aux)
    shares = lax.dot_general(
        rows, coeffs, (((1,), (1,)), ((), ())), preferred_element_type=jnp.float32
    )
    return lax.psum_scatter(
        shares.astype(jnp.bfloat16), "pair", scatter_dimension=0, tiled=True
    ).astype(jnp.float32)


def body(n_pair, n_aux, b_built, trial, energy_gap, block_live):
    blocks = trial.shape[0] // BLK
    aux = lax.axis_index("aux")
    if n_pair == 4:
        return on_four(n_aux, b_built[0], trial, energy_gap, block_live)
    own_blocks = lax.dynamic_slice_in_dim(block_live, aux * blocks, blocks, 0)
    own_live = jnp.repeat(own_blocks, BLK)
    masked = trial * own_live.astype(jnp.bfloat16)[:, None]
    response = gathered(masked, b_built[0], n_aux)
    base = energy_gap[:, None] * trial.astype(jnp.float32)
    return (base + 2.0 * own_live.astype(jnp.float32)[:, None] * response).astype(jnp.bfloat16)


def solution(mesh):
    sizes = [mesh.shape[axis] for axis in ("pair", "aux")]
    return jax.shard_map(
        functools.partial(body, *sizes),
        mesh=mesh,
        in_specs=(
            P(("traj", "aux"), None, None, "pair"),
            P(("traj", "pair", "aux"), "root"),
            P(("traj", "pair", "aux")),
            P(("traj", "pair")),
        ),
        out_specs=P(("traj", "pair", "aux"), "root"),
        check_vma=False,
    )
```

```python
import functools

import jax
import jax.numpy as jnp
from jax import lax
from jax.experimental import pallas as pl
from jax.experimental.pallas import tpu as pltpu
from jax.sharding import PartitionSpec as P

BLK = 128
V_PARTS = 2

SMEM = pl.BlockSpec(memory_space=pltpu.SMEM)
VMEM = pl.BlockSpec(memory_space=pltpu.VMEM)
ANY = pl.BlockSpec(memory_space=pl.ANY)


def contract_rows(left, right):
    return lax.dot_general(
        left, right, (((0,), (0,)), ((), ())), preferred_element_type=jnp.float32
    )


def exchange_sum(partial, n_aux):
    sent = partial.astype(jnp.bfloat16)
    if n_aux == 1:
        return sent
    if n_aux == 2:
        other = lax.ppermute(sent, "aux", [(0, 1), (1, 0)])
        return (partial + other.astype(jnp.float32)).astype(jnp.bfloat16)
    return lax.psum(sent, "aux")


def block_rows(block):
    return pl.ds(pl.multiple_of(block * BLK, BLK), BLK)


def pack_trial_kernel(at_ref, live_ref, trial_ref, *out_refs):
    width = out_refs[0].shape[1]
    for out in out_refs:
        out[...] = jnp.zeros_like(out)
    slot = jnp.int32(0)
    blocks = trial_ref.shape[0] // BLK
    for block in range(blocks):
        here = live_ref[at_ref[1] * blocks + block]

        @pl.when(here > 0)
        def _(slot=slot, block=block):
            for part, out in enumerate(out_refs):
                out[block_rows(slot), :] = trial_ref[
                    pl.ds(block * BLK, BLK), pl.ds(part * width, width)
                ]

        slot = slot + here


def plan_kernel(classes, at_ref, own_ref, near_ref, far_ref, opposite_ref, live_ref, pairs_ref, which_ref, large_ref):
    blocks = live_ref.shape[1]
    me = at_ref[0]

    def most(ref):
        top = jnp.int32(0)
        for group in range(ref.shape[0] // blocks):
            count = ref[group * blocks]
            for block in range(1, blocks):
                count = count + ref[group * blocks + block]
            top = jnp.maximum(top, count)
        return top

    alike = jnp.maximum(most(own_ref), most(opposite_ref))
    unlike = jnp.maximum(most(near_ref), most(far_ref))
    end = (me == 0) | (me == 3)
    ends_large = jnp.where(end, alike, unlike) >= jnp.where(end, unlike, alike)
    large = end == ends_large
    large_ref[0] = large.astype(jnp.int32)
    top, other = jnp.maximum(alike, unlike), jnp.minimum(alike, unlike)
    which = jnp.int32(len(classes) - 1)
    for at in range(len(classes) - 2, -1, -1):
        which = jnp.where((top <= classes[at][0]) & (other <= classes[at][1]), at, which)
    which_ref[0] = which
    rows = (((own_ref, 0), (far_ref, 2)), ((far_ref, 2), (own_ref, 0)), ((opposite_ref, 3), (near_ref, 1)), ((near_ref, 1), (opposite_ref, 3)))
    for row, ((if_large, large_flip), (if_small, small_flip)) in enumerate(rows):
        pairs_ref[row] = me ^ jnp.where(large, large_flip, small_flip)
        for block in range(blocks):
            at = at_ref[1] * blocks + block
            live_ref[row, block] = jnp.where(large, if_large[at], if_small[at])


def pack_factors_kernel(most, rest, large_ref, live_ref, pairs_ref, factors_ref, *refs):
    outs, (index_ref, sems) = refs[:4], refs[4:]
    blocks = live_ref.shape[1]
    for row in range(4):
        for slot in range(blocks):
            index_ref[row, slot] = 0
        at = jnp.int32(0)
        for block in range(blocks):
            index_ref[row, at] = block
            at = at + live_ref[row, block]
    large = large_ref[0]
    turned = 2 * (1 - large)
    rows = ((0, 1), (2, 3), (turned, 3 - turned), (2 - turned, 1 + turned))
    copies = []
    for at, (out, pieces) in enumerate(zip(outs, rows)):
        for piece, (row, start, slots) in enumerate(zip(pieces, (0, most), (most, rest))):
            for slot in range(slots):
                copies.append(
                    pltpu.make_async_copy(
                        factors_ref.at[pairs_ref[row], block_rows(index_ref[row, slot]), :],
                        out.at[pl.ds((start + slot) * BLK, BLK), :],
                        sems.at[2 * at + piece, slot],
                    )
                )
                copies[-1].start()
    for copy in copies:
        copy.wait()


def base_kernel(gap_ref, trial_ref, *out_refs):
    width = out_refs[0].shape[1]
    for block in range(trial_ref.shape[0] // BLK):
        rows = pl.ds(block * BLK, BLK)
        gap = jnp.transpose(jnp.broadcast_to(gap_ref[pl.ds(block, 1), :], (width, BLK)))
        for part, out in enumerate(out_refs):
            out[rows, :] = gap * trial_ref[rows, pl.ds(part * width, width)].astype(jnp.float32)


def finish_kernel(most, large_ref, live_ref, base_ref, sum_ref, far_ref, *refs):
    out_ref = refs[-1]
    large = large_ref[0]
    start = (1 - large) * most
    slot = jnp.int32(0)
    for block in range(out_ref.shape[0] // BLK):
        rows = pl.ds(block * BLK, BLK)
        here = jnp.where(large > 0, live_ref[0, block], live_ref[1, block])

        @pl.when(here > 0)
        def _(slot=slot, rows=rows):
            response = sum_ref[block_rows(start + slot), :] + far_ref[block_rows(slot), :].astype(jnp.float32)
            out_ref[rows, :] = (base_ref[rows, :] + 2.0 * response).astype(out_ref.dtype)

        @pl.when(here == 0)
        def _(rows=rows):
            out_ref[rows, :] = base_ref[rows, :].astype(out_ref.dtype)

        slot = slot + here


NEAR = [(z, z ^ 1) for z in range(4)]
FAR = [(z, z ^ 2) for z in range(4)]


def room(mebibytes):
    return pltpu.CompilerParams(vmem_limit_bytes=mebibytes * 2**20)


def after(value, *others):
    return lax.optimization_barrier((value, *others))[0]


def along_line(most, rest, n_aux, large, live, pairs, trial, gap, factors, owns):
    rows, vecs = trial.shape
    width = vecs // V_PARTS
    is_large = large[0] > 0
    cut = most * BLK
    held = cut + rest * BLK
    owns = [own[:cut] for own in owns]
    steps = ((FAR, NEAR), (NEAR, FAR))

    def side(own, got):
        return jnp.concatenate(
            [jnp.where(is_large, own, got), jnp.where(is_large, got, own)[: held - cut]]
        )

    firsts = [lax.ppermute(own, "pair", step[0]) for own, step in zip(owns, steps)]
    packed = pl.pallas_call(
        functools.partial(pack_factors_kernel, most, rest),
        out_shape=[jax.ShapeDtypeStruct((held, factors.shape[2]), factors.dtype)] * 4,
        in_specs=[SMEM, SMEM, SMEM, ANY],
        out_specs=[VMEM] * 4,
        scratch_shapes=[
            pltpu.SMEM((4, rows // BLK), jnp.int32),
            pltpu.SemaphoreType.DMA((8, most)),
        ],
        compiler_params=room(12),
        name="pack_factors",
    )(large, live, pairs, factors)
    bases = pl.pallas_call(
        base_kernel,
        out_shape=[jax.ShapeDtypeStruct((rows, width), jnp.float32)] * V_PARTS,
        in_specs=[VMEM, VMEM],
        out_specs=[VMEM] * V_PARTS,
        compiler_params=room(4),
        name="base",
    )(gap, trial)
    mine = [after(side(own, got), *packed) for own, got in zip(owns, firsts)]
    theirs = [lax.ppermute(held_here, "pair", step[1]) for held_here, step in zip(mine, steps)]
    theirs[1] = after(theirs[1], *bases)

    totals, aways = [None] * V_PARTS, [None] * V_PARTS
    partial = None
    for part in reversed(range(V_PARTS)):
        own_factors, other_factors = packed[2 * part : 2 * part + 2]
        got = theirs[part] if partial is None else after(theirs[part], partial)
        partial = contract_rows(mine[part], own_factors) + contract_rows(got, other_factors)
        coeffs = exchange_sum(partial, n_aux)

        def share(of):
            return lax.dot_general(
                of, coeffs, (((1,), (1,)), ((), ())), preferred_element_type=jnp.float32
            )

        got = lax.ppermute(share(other_factors).astype(jnp.bfloat16), "pair", steps[part][1])
        totals[part] = total = share(own_factors) + got.astype(jnp.float32)
        for_small = total[cut:]
        if most > rest:
            for_small = jnp.pad(for_small, ((0, 2 * cut - held), (0, 0)))
        aways[part] = jnp.where(is_large, for_small, total[:cut]).astype(jnp.bfloat16)
    aways[0] = after(aways[0], aways[1])
    sigma = None
    for part in reversed(range(V_PARTS)):
        got = lax.ppermute(aways[part], "pair", steps[part][0])
        begun = sigma is not None
        sigma = pl.pallas_call(
            functools.partial(finish_kernel, most),
            out_shape=jax.ShapeDtypeStruct((rows, vecs), trial.dtype),
            grid=(1,),
            in_specs=[SMEM, SMEM, VMEM, VMEM, VMEM] + ([ANY] if begun else []),
            out_specs=pl.BlockSpec((rows, width), lambda _, part=part: (0, part)),
            input_output_aliases={5: 0} if begun else {},
            compiler_params=room(6),
            name="finish",
        )(large, live, bases[part], totals[part], got, *([sigma] if begun else []))
    return sigma


def on_four(n_aux, factors, trial, energy_gap, block_live):
    rows, vecs = trial.shape
    blocks = rows // BLK
    classes = [pair for pair in ((5, 3), (6, 3), (6, 4), (7, 3), (7, 4)) if max(pair) < blocks] + [(blocks, blocks)]
    at = jnp.stack([lax.axis_index("pair"), lax.axis_index("aux")]).astype(jnp.int32)
    flags = [block_live] + [
        lax.ppermute(block_live, "pair", [(z, z ^ flip) for z in range(4)]) for flip in range(1, 4)
    ]
    owns = pl.pallas_call(
        pack_trial_kernel,
        out_shape=[jax.ShapeDtypeStruct((rows, vecs // V_PARTS), trial.dtype)] * V_PARTS,
        in_specs=[SMEM, SMEM, VMEM],
        out_specs=[VMEM] * V_PARTS,
        compiler_params=room(4),
        name="pack_trial",
    )(at, block_live, trial)
    live, pairs, which, large = pl.pallas_call(
        functools.partial(plan_kernel, classes),
        out_shape=[
            jax.ShapeDtypeStruct((4, blocks), jnp.int32),
            jax.ShapeDtypeStruct((4,), jnp.int32),
            jax.ShapeDtypeStruct((1,), jnp.int32),
            jax.ShapeDtypeStruct((1,), jnp.int32),
        ],
        in_specs=[SMEM] * 5,
        out_specs=[SMEM] * 4,
        compiler_params=room(2),
        name="plan",
    )(at, *flags)
    return lax.switch(
        which[0],
        [functools.partial(along_line, *pair, n_aux) for pair in classes],
        large,
        live,
        pairs,
        trial,
        energy_gap.reshape(blocks, BLK),
        factors,
        owns,
    )


def gathered(masked, factors, n_aux):
    everyone = lax.all_gather(masked, "pair", axis=0, tiled=True)
    rows = factors.reshape(-1, factors.shape[2])
    coeffs = exchange_sum(contract_rows(everyone, rows), n_aux)
    shares = lax.dot_general(
        rows, coeffs, (((1,), (1,)), ((), ())), preferred_element_type=jnp.float32
    )
    return lax.psum_scatter(
        shares.astype(jnp.bfloat16), "pair", scatter_dimension=0, tiled=True
    ).astype(jnp.float32)


def body(n_pair, n_aux, b_built, trial, energy_gap, block_live):
    blocks = trial.shape[0] // BLK
    aux = lax.axis_index("aux")
    if n_pair == 4:
        return on_four(n_aux, b_built[0], trial, energy_gap, block_live)
    own_blocks = lax.dynamic_slice_in_dim(block_live, aux * blocks, blocks, 0)
    own_live = jnp.repeat(own_blocks, BLK)
    masked = trial * own_live.astype(jnp.bfloat16)[:, None]
    response = gathered(masked, b_built[0], n_aux)
    base = energy_gap[:, None] * trial.astype(jnp.float32)
    return (base + 2.0 * own_live.astype(jnp.float32)[:, None] * response).astype(jnp.bfloat16)


def solution(mesh):
    sizes = [mesh.shape[axis] for axis in ("pair", "aux")]
    return jax.shard_map(
        functools.partial(body, *sizes),
        mesh=mesh,
        in_specs=(
            P(("traj", "aux"), None, None, "pair"),
            P(("traj", "pair", "aux"), "root"),
            P(("traj", "pair", "aux")),
            P(("traj", "pair")),
        ),
        out_specs=P(("traj", "pair", "aux"), "root"),
        check_vma=False,
    )
```

```python
import functools

import jax
import jax.numpy as jnp
from jax import lax
from jax.experimental import pallas as pl
from jax.experimental.pallas import tpu as pltpu
from jax.sharding import PartitionSpec as P

BLK = 128
V_PARTS = 2

SMEM = pl.BlockSpec(memory_space=pltpu.SMEM)
VMEM = pl.BlockSpec(memory_space=pltpu.VMEM)
ANY = pl.BlockSpec(memory_space=pl.ANY)


def contract_rows(left, right):
    return lax.dot_general(
        left, right, (((0,), (0,)), ((), ())), preferred_element_type=jnp.float32
    )


def exchange_sum(partial, n_aux):
    sent = partial.astype(jnp.bfloat16)
    if n_aux == 1:
        return sent
    if n_aux == 2:
        other = lax.ppermute(sent, "aux", [(0, 1), (1, 0)])
        return (partial + other.astype(jnp.float32)).astype(jnp.bfloat16)
    return lax.psum(sent, "aux")


def block_rows(block):
    return pl.ds(pl.multiple_of(block * BLK, BLK), BLK)


def pack_trial_kernel(at_ref, live_ref, trial_ref, *out_refs):
    width = out_refs[0].shape[1]
    for out in out_refs:
        out[...] = jnp.zeros_like(out)
    slot = jnp.int32(0)
    blocks = trial_ref.shape[0] // BLK
    for block in range(blocks):
        here = live_ref[at_ref[1] * blocks + block]

        @pl.when(here > 0)
        def _(slot=slot, block=block):
            for part, out in enumerate(out_refs):
                out[block_rows(slot), :] = trial_ref[
                    pl.ds(block * BLK, BLK), pl.ds(part * width, width)
                ]

        slot = slot + here


def plan_kernel(classes, at_ref, own_ref, near_ref, far_ref, opposite_ref, live_ref, pairs_ref, which_ref, large_ref):
    blocks = live_ref.shape[1]
    me = at_ref[0]

    def most(ref):
        top = jnp.int32(0)
        for group in range(ref.shape[0] // blocks):
            count = ref[group * blocks]
            for block in range(1, blocks):
                count = count + ref[group * blocks + block]
            top = jnp.maximum(top, count)
        return top

    alike = jnp.maximum(most(own_ref), most(opposite_ref))
    unlike = jnp.maximum(most(near_ref), most(far_ref))
    end = (me == 0) | (me == 3)
    ends_large = jnp.where(end, alike, unlike) >= jnp.where(end, unlike, alike)
    large = end == ends_large
    large_ref[0] = large.astype(jnp.int32)
    top, other = jnp.maximum(alike, unlike), jnp.minimum(alike, unlike)
    which = jnp.int32(len(classes) - 1)
    for at in range(len(classes) - 2, -1, -1):
        which = jnp.where((top <= classes[at][0]) & (other <= classes[at][1]), at, which)
    which_ref[0] = which
    rows = (((own_ref, 0), (far_ref, 2)), ((far_ref, 2), (own_ref, 0)), ((opposite_ref, 3), (near_ref, 1)), ((near_ref, 1), (opposite_ref, 3)))
    for row, ((if_large, large_flip), (if_small, small_flip)) in enumerate(rows):
        pairs_ref[row] = me ^ jnp.where(large, large_flip, small_flip)
        for block in range(blocks):
            at = at_ref[1] * blocks + block
            live_ref[row, block] = jnp.where(large, if_large[at], if_small[at])


def pack_factors_kernel(most, rest, large_ref, live_ref, pairs_ref, factors_ref, *refs):
    outs, (index_ref, sems) = refs[:4], refs[4:]
    blocks = live_ref.shape[1]
    for row in range(4):
        for slot in range(blocks):
            index_ref[row, slot] = 0
        at = jnp.int32(0)
        for block in range(blocks):
            index_ref[row, at] = block
            at = at + live_ref[row, block]
    large = large_ref[0]
    turned = 2 * (1 - large)
    rows = ((0, 1), (2, 3), (turned, 3 - turned), (2 - turned, 1 + turned))
    copies = []
    for at, (out, pieces) in enumerate(zip(outs, rows)):
        for piece, (row, start, slots) in enumerate(zip(pieces, (0, most), (most, rest))):
            for slot in range(slots):
                copies.append(
                    pltpu.make_async_copy(
                        factors_ref.at[pairs_ref[row], block_rows(index_ref[row, slot]), :],
                        out.at[pl.ds((start + slot) * BLK, BLK), :],
                        sems.at[2 * at + piece, slot],
                    )
                )
                copies[-1].start()
    for copy in copies:
        copy.wait()


def base_kernel(gap_ref, trial_ref, *out_refs):
    width = out_refs[0].shape[1]
    for block in range(trial_ref.shape[0] // BLK):
        rows = pl.ds(block * BLK, BLK)
        gap = jnp.transpose(jnp.broadcast_to(gap_ref[pl.ds(block, 1), :], (width, BLK)))
        for part, out in enumerate(out_refs):
            out[rows, :] = gap * trial_ref[rows, pl.ds(part * width, width)].astype(jnp.float32)


def finish_kernel(most, large_ref, live_ref, base_ref, sum_ref, far_ref, *refs):
    out_ref = refs[-1]
    large = large_ref[0]
    start = (1 - large) * most
    slot = jnp.int32(0)
    for block in range(out_ref.shape[0] // BLK):
        rows = pl.ds(block * BLK, BLK)
        here = jnp.where(large > 0, live_ref[0, block], live_ref[1, block])

        @pl.when(here > 0)
        def _(slot=slot, rows=rows):
            response = sum_ref[block_rows(start + slot), :] + far_ref[block_rows(slot), :].astype(jnp.float32)
            out_ref[rows, :] = (base_ref[rows, :] + 2.0 * response).astype(out_ref.dtype)

        @pl.when(here == 0)
        def _(rows=rows):
            out_ref[rows, :] = base_ref[rows, :].astype(out_ref.dtype)

        slot = slot + here


NEAR = [(z, z ^ 1) for z in range(4)]
FAR = [(z, z ^ 2) for z in range(4)]


def room(mebibytes):
    return pltpu.CompilerParams(vmem_limit_bytes=mebibytes * 2**20)


def after(value, *others):
    return lax.optimization_barrier((value, *others))[0]


def along_line(most, rest, n_aux, large, live, pairs, trial, gap, factors, owns):
    rows, vecs = trial.shape
    width = vecs // V_PARTS
    is_large = large[0] > 0
    cut = most * BLK
    held = cut + rest * BLK
    owns = [own[:cut] for own in owns]
    steps = ((FAR, NEAR), (NEAR, FAR))

    def side(own, got):
        return jnp.concatenate(
            [jnp.where(is_large, own, got), jnp.where(is_large, got, own)[: held - cut]]
        )

    firsts = [lax.ppermute(own, "pair", step[0]) for own, step in zip(owns, steps)]
    packed = pl.pallas_call(
        functools.partial(pack_factors_kernel, most, rest),
        out_shape=[jax.ShapeDtypeStruct((held, factors.shape[2]), factors.dtype)] * 4,
        in_specs=[SMEM, SMEM, SMEM, ANY],
        out_specs=[VMEM] * 4,
        scratch_shapes=[
            pltpu.SMEM((4, rows // BLK), jnp.int32),
            pltpu.SemaphoreType.DMA((8, most)),
        ],
        compiler_params=room(12),
        name="pack_factors",
    )(large, live, pairs, factors)
    bases = pl.pallas_call(
        base_kernel,
        out_shape=[jax.ShapeDtypeStruct((rows, width), jnp.float32)] * V_PARTS,
        in_specs=[VMEM, VMEM],
        out_specs=[VMEM] * V_PARTS,
        compiler_params=room(4),
        name="base",
    )(gap, trial)
    mine = [after(side(own, got), *packed) for own, got in zip(owns, firsts)]
    theirs = [lax.ppermute(held_here, "pair", step[1]) for held_here, step in zip(mine, steps)]
    theirs[1] = after(theirs[1], *bases)

    totals, aways = [None] * V_PARTS, [None] * V_PARTS
    partial = None
    for part in reversed(range(V_PARTS)):
        own_factors, other_factors = packed[2 * part : 2 * part + 2]
        got = theirs[part] if partial is None else after(theirs[part], partial)
        partial = contract_rows(mine[part], own_factors) + contract_rows(got, other_factors)
        coeffs = exchange_sum(partial, n_aux)

        def share(of):
            return lax.dot_general(
                of, coeffs, (((1,), (1,)), ((), ())), preferred_element_type=jnp.float32
            )

        got = lax.ppermute(share(other_factors).astype(jnp.bfloat16), "pair", steps[part][1])
        totals[part] = total = share(own_factors) + got.astype(jnp.float32)
        for_small = total[cut:]
        if most > rest:
            for_small = jnp.pad(for_small, ((0, 2 * cut - held), (0, 0)))
        aways[part] = jnp.where(is_large, for_small, total[:cut]).astype(jnp.bfloat16)
    aways[0] = after(aways[0], aways[1])
    sigma = None
    for part in reversed(range(V_PARTS)):
        got = lax.ppermute(aways[part], "pair", steps[part][0])
        begun = sigma is not None
        sigma = pl.pallas_call(
            functools.partial(finish_kernel, most),
            out_shape=jax.ShapeDtypeStruct((rows, vecs), trial.dtype),
            grid=(1,),
            in_specs=[SMEM, SMEM, VMEM, VMEM, VMEM] + ([ANY] if begun else []),
            out_specs=pl.BlockSpec((rows, width), lambda _, part=part: (0, part)),
            input_output_aliases={5: 0} if begun else {},
            compiler_params=room(6),
            name="finish",
        )(large, live, bases[part], totals[part], got, *([sigma] if begun else []))
    return sigma


def on_four(n_aux, factors, trial, energy_gap, block_live):
    rows, vecs = trial.shape
    blocks = rows // BLK
    classes = [pair for pair in ((5, 3), (6, 3), (6, 4), (7, 3), (7, 4), (8, 5)) if max(pair) <= blocks] + [(blocks, blocks)]
    at = jnp.stack([lax.axis_index("pair"), lax.axis_index("aux")]).astype(jnp.int32)
    flags = [block_live] + [
        lax.ppermute(block_live, "pair", [(z, z ^ flip) for z in range(4)]) for flip in range(1, 4)
    ]
    owns = pl.pallas_call(
        pack_trial_kernel,
        out_shape=[jax.ShapeDtypeStruct((rows, vecs // V_PARTS), trial.dtype)] * V_PARTS,
        in_specs=[SMEM, SMEM, VMEM],
        out_specs=[VMEM] * V_PARTS,
        compiler_params=room(4),
        name="pack_trial",
    )(at, block_live, trial)
    live, pairs, which, large = pl.pallas_call(
        functools.partial(plan_kernel, classes),
        out_shape=[
            jax.ShapeDtypeStruct((4, blocks), jnp.int32),
            jax.ShapeDtypeStruct((4,), jnp.int32),
            jax.ShapeDtypeStruct((1,), jnp.int32),
            jax.ShapeDtypeStruct((1,), jnp.int32),
        ],
        in_specs=[SMEM] * 5,
        out_specs=[SMEM] * 4,
        compiler_params=room(2),
        name="plan",
    )(at, *flags)
    return lax.switch(
        which[0],
        [functools.partial(along_line, *pair, n_aux) for pair in classes],
        large,
        live,
        pairs,
        trial,
        energy_gap.reshape(blocks, BLK),
        factors,
        owns,
    )


def gathered(masked, factors, n_aux):
    everyone = lax.all_gather(masked, "pair", axis=0, tiled=True)
    rows = factors.reshape(-1, factors.shape[2])
    coeffs = exchange_sum(contract_rows(everyone, rows), n_aux)
    shares = lax.dot_general(
        rows, coeffs, (((1,), (1,)), ((), ())), preferred_element_type=jnp.float32
    )
    return lax.psum_scatter(
        shares.astype(jnp.bfloat16), "pair", scatter_dimension=0, tiled=True
    ).astype(jnp.float32)


def body(n_pair, n_aux, b_built, trial, energy_gap, block_live):
    blocks = trial.shape[0] // BLK
    aux = lax.axis_index("aux")
    if n_pair == 4:
        return on_four(n_aux, b_built[0], trial, energy_gap, block_live)
    own_blocks = lax.dynamic_slice_in_dim(block_live, aux * blocks, blocks, 0)
    own_live = jnp.repeat(own_blocks, BLK)
    masked = trial * own_live.astype(jnp.bfloat16)[:, None]
    response = gathered(masked, b_built[0], n_aux)
    base = energy_gap[:, None] * trial.astype(jnp.float32)
    return (base + 2.0 * own_live.astype(jnp.float32)[:, None] * response).astype(jnp.bfloat16)


def solution(mesh):
    sizes = [mesh.shape[axis] for axis in ("pair", "aux")]
    return jax.shard_map(
        functools.partial(body, *sizes),
        mesh=mesh,
        in_specs=(
            P(("traj", "aux"), None, None, "pair"),
            P(("traj", "pair", "aux"), "root"),
            P(("traj", "pair", "aux")),
            P(("traj", "pair")),
        ),
        out_specs=P(("traj", "pair", "aux"), "root"),
        check_vma=False,
    )
```
